32 devices in a mesh: head: 4 (over z), seq: 8 (over y, x, core).
Axes of the slice: x: 2, y: 2, z: 4, core: 2. Of those that a mesh axis runs over, the one named last changes fastest.
Arguments:
- query_mla: bfloat16 [256, 24576], P(None, 'head'), may hold values from -6 to 6
- key_mla: bfloat16 [4096, 24576], P('seq', 'head'), may hold values from -6 to 6
- lse: float32 [256, 128], P(None, 'head'), may hold values from 3 to 6
- query_index: bfloat16 [256, 8192], P(None, 'head'), may hold values from -0.5 to 0.5
- key_index: bfloat16 [4096, 128], P('seq'), may hold values from -6 to 6
- head_weight: float32 [256, 64], P(None, 'head'), may hold values from -25 to 25
- query_pos: int32 [256], replicated, may hold values from 1024 to 4095
- key_block: int32 [8], P('seq'), may hold values from 0 to 7, each once
Outputs:
- kl: bfloat16 [256], replicated
- grad_query_index: bfloat16 [256, 8192], P(None, 'head')
- grad_head_weight: bfloat16 [256, 64], P(None, 'head')
- grad_key_index: bfloat16 [4096, 128], P('seq')
The draws below stay inside these ranges and needn't reach their ends.
Inputs may be any that keep to these rules, and one draw needn't show every extreme that they name: key_block is a permutation of 0 to 7; the keys of index d of seq hold the positions key_block[d] * 512 to key_block[d] * 512 + 511.
All inputs are finite; a program needn't handle non-finite values.
Results may differ from the reference program's by a relative error of at most 0.012.
Values may be sent and summed in bfloat16 or wider, within the bound.
No kernel may reach another device: no remote copies, remote signals or barrier semaphores. Data moves between devices by JAX's collectives and lax.ppermute only.
A program may use at most 128 MiB of HBM per device.

```python
import jax
import jax.numpy as jnp
from jax import lax

H = 128
DQK = 192
HI = 64
DI = 128
ROWS = 256
KEY_DEV = 512
CONTEXT = 4096
N_SEQ = 8


def draw_head_weight(key, part):
    base_key = jax.random.fold_in(key, 11)
    return jnp.clip(0.75 * jax.random.normal(base_key, (ROWS, HI), jnp.float32), -2.25, 2.25)


def place_ends(values, stream_key, low, largest):
    index_at = [jax.random.randint(jax.random.fold_in(stream_key, axis), (), 0, length) for axis, length in enumerate(values.shape)]
    longest = values.shape.index(max(values.shape))
    beside = index_at[:longest] + [(index_at[longest] + 1) % values.shape[longest]] + index_at[longest + 1:]
    return values.at[tuple(index_at)].set(low).at[tuple(beside)].set(largest)


def shard_levels(rng, shape, cuts, least, top_value):
    gain = 1.0
    for dim, shards_of in cuts:
        steps = jax.random.uniform(jax.random.fold_in(jax.random.fold_in(rng, 6), dim), (shards_of,), jnp.float32, least / len(cuts), top_value / len(cuts))
        gain = gain * jnp.repeat(jnp.exp(steps), shape[dim] // shards_of).reshape((-1,) + (1,) * (len(shape) - 1 - dim))
    return gain


def noise(key, extent, spread, limit, shards=(), kind=jnp.bfloat16):
    values = jax.random.normal(key, extent, jnp.float32) * spread
    if len(shards) > 0:
        values = shard_levels(key, extent, shards, -0.22, 0.18) * values
    return jnp.clip(values, min=-limit, max=limit).astype(kind)


def setup_inputs(seed: int = 0) -> dict:
    seeds = jax.random.split(jax.random.key(seed), 9)
    query_mla = noise(seeds[0], (ROWS, H * DQK), 1.0, 6.0, ((1, 4),))
    key_mla = noise(seeds[1], (CONTEXT, H * DQK), 1.0, 6.0, ((0, 8), (1, 4)))
    lse = jnp.clip(3.0 + 3.0 * jax.random.uniform(seeds[2], (ROWS, H), jnp.float32) ** shard_levels(seeds[2], (ROWS, H), ((1, 4),), -0.2, 0.2), 3.0, 6.0)
    query_index = noise(seeds[3], (ROWS, HI * DI), DI ** -0.5, 0.5, ((1, 4),))
    key_index = noise(seeds[4], (CONTEXT, DI), 1.0, 6.0, ((0, 8),))
    head_weight = draw_head_weight(jax.random.fold_in(seeds[8], 71), 0)
    query_pos = place_ends(jax.random.randint(seeds[6], (ROWS,), CONTEXT // 4, CONTEXT), jax.random.fold_in(seeds[6], 1), CONTEXT // 4, CONTEXT - 1).astype(jnp.int32)
    key_block = jax.random.permutation(seeds[7], N_SEQ).astype(jnp.int32)
    return {"query_mla": query_mla, "key_mla": key_mla, "lse": lse, "query_index": query_index, "key_index": key_index, "head_weight": head_weight, "query_pos": query_pos, "key_block": key_block}


def reference(query_mla, key_mla, lse, query_index, key_index, head_weight, query_pos, key_block):
    positions = (jnp.repeat(key_block, KEY_DEV) * KEY_DEV + jnp.tile(jnp.arange(KEY_DEV, dtype=jnp.int32), N_SEQ)).astype(jnp.int32)
    valid = positions[None, :] <= query_pos[:, None]
    queries = query_mla.reshape(ROWS, H, DQK)
    mla_keys = key_mla.reshape(CONTEXT, H, DQK)

    def add_head(carried, head_index):
        q_head = lax.dynamic_index_in_dim(queries, head_index, 1, keepdims=False)
        k_head = lax.dynamic_index_in_dim(mla_keys, head_index, 1, keepdims=False)
        score = jnp.dot(q_head, k_head.T, preferred_element_type=jnp.float32) * (DQK ** -0.5)
        shifts = lax.dynamic_index_in_dim(lse, head_index, 1, keepdims=False)
        return carried + jnp.where(valid, jnp.exp(score - shifts[:, None]), 0.0), None

    attention, _ = lax.scan(add_head, jnp.zeros((ROWS, CONTEXT), jnp.float32), jnp.arange(H, dtype=jnp.int32))
    indexer_q = query_index.reshape(ROWS, HI, DI)

    def index_dots(head_index):
        q_head = lax.dynamic_index_in_dim(indexer_q, head_index, 1, keepdims=False)
        return jnp.dot(q_head, key_index.T, preferred_element_type=jnp.float32), q_head

    def add_logit(carried, head_index):
        dots, _ = index_dots(head_index)
        weights = lax.dynamic_index_in_dim(head_weight, head_index, 1, keepdims=False)
        return carried + weights[:, None] * jnp.maximum(dots, 0.0), None

    logit, _ = lax.scan(add_logit, jnp.zeros((ROWS, CONTEXT), jnp.float32), jnp.arange(HI, dtype=jnp.int32))
    total = jnp.sum(attention, axis=1)
    target = attention / total[:, None]
    masked = jnp.where(valid, logit, -1e30)
    peak = jnp.max(masked, axis=1)
    norm = jnp.sum(jnp.where(valid, jnp.exp(masked - peak[:, None]), 0.0), axis=1)
    log_prob = masked - peak[:, None] - jnp.log(norm)[:, None]
    prob = jnp.where(valid, jnp.exp(log_prob), 0.0)
    log_target = jnp.log(jnp.where(valid, attention, 1.0)) - jnp.log(total)[:, None]
    kl = jnp.sum(jnp.where(valid, target * (log_target - log_prob), 0.0), axis=1).astype(jnp.bfloat16)
    dlogit = jnp.where(valid, prob - target, 0.0).astype(jnp.bfloat16)
    grad_rows = dlogit.astype(jnp.float32)

    def backward(carried, head_index):
        dots, q_head = index_dots(head_index)
        weights = lax.dynamic_index_in_dim(head_weight, head_index, 1, keepdims=False)
        grad_weight = jnp.sum(grad_rows * jnp.maximum(dots, 0.0), axis=1)
        opened = dots > 0
        gated = jnp.where(opened, dlogit, 0).astype(jnp.bfloat16)
        grad_query = jnp.dot(gated, key_index, preferred_element_type=jnp.float32) * weights[:, None]
        coef = jnp.where(opened, grad_rows * weights[:, None], 0.0).astype(jnp.bfloat16)
        grad_key = carried + jnp.dot(coef.T, q_head, preferred_element_type=jnp.float32)
        return grad_key, (grad_weight, grad_query)

    grad_key, (grad_weights, grad_queries) = lax.scan(backward, jnp.zeros((CONTEXT, DI), jnp.float32), jnp.arange(HI, dtype=jnp.int32))
    grad_head_weight = grad_weights.T.astype(jnp.bfloat16)
    grad_query_index = jnp.transpose(grad_queries, (1, 0, 2)).reshape(ROWS, HI * DI).astype(jnp.bfloat16)
    return kl, grad_query_index, grad_head_weight, grad_key.astype(jnp.bfloat16)
```

```python
import functools
import math

import jax
import jax.numpy as jnp
from jax import lax
from jax.experimental import pallas as pl
from jax.experimental.pallas import tpu as pltpu
from jax.sharding import PartitionSpec as P

BF16 = jnp.bfloat16
F32 = jnp.float32
LANES = 128
NT = (((1,), (1,)), ((), ()))


def vmem_spec():
    return pl.BlockSpec(memory_space=pltpu.VMEM)


def smem_spec():
    return pl.BlockSpec(memory_space=pltpu.SMEM)


def bits(n):
    return [1 << b for b in range(n.bit_length() - 1)]


def attention_kernel(heads_step, width, split, me_ref, block_ref, q_ref, k_ref, lse_ref, qi_ref, hw_ref, out_ref, acc_ref):
    step = pl.program_id(0)
    rows, keys = q_ref.shape[0], k_ref.shape[0]
    log2e = math.log2(math.e)
    scale = width ** (-0.5) * log2e
    lanes = lax.broadcasted_iota(jnp.int32, lse_ref.shape, 1)
    total = None
    for a in range(heads_step):
        low, high = a * width, (a + 1) * width
        start = low // LANES * LANES
        stop = -(-high // LANES) * LANES
        q = q_ref[:, start:stop]
        if start != low or stop != high:
            at = lax.broadcasted_iota(jnp.int32, q.shape, 1) + start
            q = jnp.where((at >= low) & (at < high), q, jnp.zeros_like(q))
        score = lax.dot_general(q, k_ref[:, start:stop], NT, preferred_element_type=F32)
        shift = jnp.sum(jnp.where(lanes == step * heads_step + a, lse_ref[...], 0.0), axis=1, keepdims=True) * log2e
        value = jnp.exp2(score * scale - shift)
        total = value if total is None else total + value

    @pl.when(step == 0)
    def _():
        acc_ref[...] = total

    @pl.when(step > 0)
    def _():
        acc_ref[...] += total

    @pl.when(step == pl.num_programs(0) - 1)
    def _():
        out_ref[:, :keys] = acc_ref[...].astype(BF16)
        cols = qi_ref.shape[1] // split
        out_ref[:, keys : keys + cols] = qi_ref[:, pl.ds(pl.multiple_of(me_ref[0] * cols, LANES), cols)]
        n = hw_ref.shape[1]
        weight = hw_ref[...]
        high = weight.astype(BF16)
        rest = weight - high.astype(F32)
        mid = rest.astype(BF16)
        low = (rest - mid.astype(F32)).astype(BF16)
        row = lax.broadcasted_iota(jnp.int32, (n, LANES), 0)
        col = lax.broadcasted_iota(jnp.int32, (n, LANES), 1)
        side = jnp.where(
            lax.broadcasted_iota(jnp.int32, (rows, LANES), 1) == 3 * n, block_ref[0].astype(F32), 0.0
        )
        for e, term in enumerate((high, mid, low)):
            place = jnp.where(col == row + e * n, 1.0, 0.0).astype(BF16)
            side = side + jnp.dot(term, place, preferred_element_type=F32)
        out_ref[:, keys + cols :] = side.astype(BF16)


def rows_kernel(n_seq, n_head, own, me_ref, pos_ref, got_ref, *refs):
    key_refs = refs[:n_seq]
    gq_refs = refs[n_seq : n_seq + n_head]
    near_ref, far_ref = refs[n_seq + n_head : n_seq + n_head + 2]
    (keys_ref, q_ref, wide_ref, dots_ref, logit_ref, att_ref, valid_ref, dl_ref, gq_ref) = refs[n_seq + n_head + 2 :]
    s, h = me_ref[0], me_ref[1]
    keys, width = key_refs[0].shape
    heads_all = q_ref.shape[0] // own
    heads = heads_all // n_head
    per = heads // n_seq
    cols = per * width
    group = n_head * own
    for k in range(n_seq):
        keys_ref[k] = key_refs[k][...]
    for hh in range(n_head):
        for ss in range(n_seq):
            at = (ss * n_head + hh) * own
            base = at // (2 * own) * 2 * own
            both = got_ref[base : base + 2 * own, keys : keys + cols].astype(F32)
            part = both[at - base : at - base + own]
            tiles = [part[:, e * width : (e + 1) * width] for e in range(per)]
            first = (hh * heads + ss * per) * own
            q_ref[first : first + per * own, :] = jnp.concatenate(tiles, axis=0).astype(BF16)
        at = hh * own
        base = at // (2 * own) * 2 * own
        side = got_ref[base : base + 2 * own, keys + cols :].astype(F32)[at - base : at - base + own]
        for i in range(heads):
            one = side[:, i : i + 1] + side[:, heads + i : heads + i + 1] + side[:, 2 * heads + i : 2 * heads + i + 1]
            wide_ref[hh * heads + i] = jnp.broadcast_to(one, (own, LANES))
    first_row = (s * n_head + h) * own
    sub = lax.broadcasted_iota(jnp.int32, (own, keys), 0)
    place = jnp.zeros((own, keys), F32)
    for t in range(own):
        place = jnp.where(sub == t, pos_ref[first_row + t].astype(F32), place)
    lane = lax.broadcasted_iota(jnp.int32, (own, keys), 1).astype(F32)

    def forward(k, peak):
        dots = lax.dot_general(q_ref[...], keys_ref[k], NT, preferred_element_type=F32)
        dots_ref[k] = dots.astype(BF16)
        cube = jnp.maximum(dots, 0.0).reshape(heads_all, own, keys)
        parts = []
        for c in range(keys // LANES):
            parts.append(jnp.sum(cube[:, :, c * LANES : (c + 1) * LANES] * wide_ref[...], axis=0))
        logit = jnp.concatenate(parts, axis=1)
        src = pl.multiple_of((s ^ k) * group, group)
        share = got_ref[pl.ds(src, group), :keys].astype(F32).reshape(n_head, own, keys)
        side = got_ref[pl.ds(src, 2 * own), keys + cols :].astype(F32)
        block = side[:own, 3 * heads : 3 * heads + 1]
        valid = block * float(keys) + lane <= place
        logit = jnp.where(valid, logit, -1e30)
        logit_ref[k] = logit
        att_ref[k] = jnp.where(valid, jnp.sum(share, axis=0), 0.0)
        valid_ref[k] = jnp.where(valid, 1.0, 0.0)
        return jnp.maximum(peak, jnp.max(logit, axis=1, keepdims=True))

    peak = lax.fori_loop(0, n_seq, forward, jnp.full((own, 1), -1e30, F32))
    valid = valid_ref[...] > 0.0
    att = att_ref[...]
    logit = logit_ref[...]

    def row_sum(x):
        return jnp.sum(jnp.sum(x, axis=0), axis=1, keepdims=True)

    total = row_sum(att)
    shifted = jnp.where(valid, jnp.exp(logit - peak[None]), 0.0)
    norm = row_sum(shifted)
    target = att / total[None]
    log_prob = logit - peak[None] - jnp.log(norm)[None]
    prob = jnp.where(valid, jnp.exp(log_prob), 0.0)
    log_target = jnp.log(jnp.where(valid, att, 1.0)) - jnp.log(total)[None]
    kl = row_sum(jnp.where(valid, target * (log_target - log_prob), 0.0))
    dl = jnp.where(valid, prob - target, 0.0)
    dl_ref[...] = jnp.concatenate([dl, dl], axis=1).astype(BF16)
    wide = wide_ref[...].reshape(heads_all * own, LANES)
    weighted = jnp.transpose(q_ref[...].astype(F32) * wide).astype(BF16)

    def backward(k, _):
        dots = dots_ref[k].astype(F32).reshape(heads_all // 2, 2 * own, keys)
        one = dl_ref[k].astype(F32)[None]
        gated = jnp.where(dots > 0.0, one, 0.0).reshape(heads_all * own, keys).astype(BF16)
        term = jnp.dot(gated, keys_ref[k], preferred_element_type=F32)
        gq_ref[...] = jnp.where(k == 0, 0.0, gq_ref[...]) + term
        side = jnp.dot(weighted, gated, preferred_element_type=F32)

        @pl.when(k % 2 == 0)
        def _():
            near_ref[k // 2] = side

        @pl.when(k % 2 == 1)
        def _():
            far_ref[k // 2] = side.astype(BF16)

        return 0

    lax.fori_loop(0, n_seq, backward, 0)
    lane = lax.broadcasted_iota(jnp.int32, (own, LANES), 1)
    for m in range(n_head):
        first = pl.multiple_of((h ^ m) * heads * own, heads * own)
        term = gq_ref[pl.ds(first, heads * own), :]
        factor = wide_ref[pl.ds((h ^ m) * heads, heads)]
        query = q_ref[pl.ds(first, heads * own), :].astype(F32)
        per_head = jnp.sum(term * query, axis=1, keepdims=True).reshape(heads, own, 1)
        scaled = term.reshape(heads, own, width) * factor
        extra = jnp.where(lane == heads, kl, 0.0)
        for i in range(heads):
            gq_refs[m][:, i * width : (i + 1) * width] = scaled[i].astype(BF16)
            extra = jnp.where(lane == i, per_head[i], extra)
        gq_refs[m][:, heads * width :] = extra.astype(BF16)


def order_kernel(n_head, me_ref, *refs):
    pieces, out_ref, cube_ref = refs[:n_head], refs[n_head], refs[n_head + 1]
    h = me_ref[1]
    for m in range(n_head):
        cube_ref[h ^ m] = pieces[m][...].astype(F32)
    out_ref[...] = cube_ref[...].reshape(out_ref.shape).astype(BF16)


def place_kernel(n_seq, heads, me_ref, *refs):
    pieces = refs[:n_seq]
    kl_ref, gq_ref, hw_ref, side_ref = refs[n_seq:]
    s = me_ref[0]
    rows, cols = pieces[0].shape[0], gq_ref.shape[1]
    for k in range(n_seq):
        at = pl.ds(pl.multiple_of((s ^ k) * rows, rows), rows)
        gq_ref[at, :] = pieces[k][:, :cols]
        side_ref[at, :] = pieces[k][:, cols:].astype(F32)
    side = side_ref[...]
    hw_ref[...] = side[:, :heads].astype(BF16)
    kl_ref[...] = jnp.transpose(side)[heads : heads + 1, :].astype(BF16)


def turn_kernel(a_ref, b_ref, out_ref):
    out_ref[...] = jnp.transpose(a_ref[...] + b_ref[...].astype(F32)).astype(BF16)


def fast_local(n_seq, n_head, query_mla, key_mla, lse, query_index, key_index, head_weight, query_pos, key_block):
    rows, keys = query_mla.shape[0], key_mla.shape[0]
    mla_heads = lse.shape[1]
    mla_width = query_mla.shape[1] // mla_heads
    heads, width = head_weight.shape[1], key_index.shape[1]
    own = rows // (n_seq * n_head)
    heads_all = heads * n_head
    s, h = lax.axis_index("seq"), lax.axis_index("head")
    me = jnp.stack([s, h]).astype(jnp.int32)

    def swap(x, axis, n, mask):
        return lax.ppermute(x, axis, [(i, i ^ mask) for i in range(n)])

    key_pieces = {0: key_index}
    for k in range(2, n_seq, 2):
        key_pieces[k] = swap(key_index, "seq", n_seq, k)
    for k in range(0, n_seq, 2):
        key_pieces[k + 1] = swap(key_pieces[k], "seq", n_seq, 1)

    heads_step = 4
    cols = query_index.shape[1] // n_seq
    whole = lambda i: (0, 0)
    sent = pl.pallas_call(
        functools.partial(attention_kernel, heads_step, mla_width, n_seq),
        grid=(mla_heads // heads_step,),
        in_specs=[
            smem_spec(),
            smem_spec(),
            pl.BlockSpec((rows, heads_step * mla_width), lambda i: (0, i)),
            pl.BlockSpec((keys, heads_step * mla_width), lambda i: (0, i)),
            pl.BlockSpec(lse.shape, whole),
            pl.BlockSpec(query_index.shape, whole),
            pl.BlockSpec(head_weight.shape, whole),
        ],
        out_specs=pl.BlockSpec((rows, keys + cols + LANES), whole),
        out_shape=jax.ShapeDtypeStruct((rows, keys + cols + LANES), BF16),
        scratch_shapes=[pltpu.VMEM((rows, keys), F32)],
        compiler_params=pltpu.CompilerParams(vmem_limit_bytes=32 * 2**20),
        cost_estimate=pl.CostEstimate(
            flops=2 * rows * keys * mla_heads * mla_width,
            bytes_accessed=2 * (rows + keys) * mla_heads * mla_width,
            transcendentals=rows * keys * mla_heads,
        ),
        name="attention",
    )(me, key_block, query_mla, key_mla, lse, query_index, head_weight)
    got = lax.all_to_all(sent, ("seq", "head"), 0, 0, tiled=True)

    wide_cols = heads * width + LANES
    half = n_seq // 2
    outs = pl.pallas_call(
        functools.partial(rows_kernel, n_seq, n_head, own),
        in_specs=[smem_spec(), smem_spec()] + [vmem_spec()] * (1 + n_seq),
        out_specs=[vmem_spec()] * (n_head + 2),
        out_shape=[jax.ShapeDtypeStruct((own, wide_cols), BF16)] * n_head
        + [
            jax.ShapeDtypeStruct((half, width, keys), F32),
            jax.ShapeDtypeStruct((half, width, keys), BF16),
        ],
        scratch_shapes=[
            pltpu.VMEM((n_seq, keys, width), BF16),
            pltpu.VMEM((heads_all * own, width), BF16),
            pltpu.VMEM((heads_all, own, LANES), F32),
            pltpu.VMEM((n_seq, heads_all * own, keys), BF16),
            pltpu.VMEM((n_seq, own, keys), F32),
            pltpu.VMEM((n_seq, own, keys), F32),
            pltpu.VMEM((n_seq, own, keys), F32),
            pltpu.VMEM((n_seq, 2 * own, keys), BF16),
            pltpu.VMEM((heads_all * own, width), F32),
        ],
        compiler_params=pltpu.CompilerParams(vmem_limit_bytes=40 * 2**20),
        cost_estimate=pl.CostEstimate(
            flops=6 * own * heads_all * n_seq * keys * width, bytes_accessed=2**21, transcendentals=0
        ),
        name="rows",
    )(me, query_pos, got, *[key_pieces[k] for k in range(n_seq)])
    pieces, near, far = outs[:n_head], outs[n_head], outs[n_head + 1]

    paired = near + swap(far, "seq", n_seq, 1).astype(F32)
    mine = paired[0]
    for e in range(1, half):
        mine = mine + swap(paired[e].astype(BF16), "seq", n_seq, 2 * e).astype(F32)
    steps = bits(n_head)
    for mask in steps[:-1]:
        mine = mine + swap(mine.astype(BF16), "head", n_head, mask).astype(F32)
    last = swap(mine.astype(BF16), "head", n_head, steps[-1])
    grad_key_index = pl.pallas_call(
        turn_kernel,
        in_specs=[vmem_spec()] * 2,
        out_specs=vmem_spec(),
        out_shape=jax.ShapeDtypeStruct((keys, width), BF16),
        name="turn",
    )(mine, last)

    row_pieces = [pieces[0]] + [swap(pieces[m], "head", n_head, m) for m in range(1, n_head)]
    ordered = pl.pallas_call(
        functools.partial(order_kernel, n_head),
        in_specs=[smem_spec()] + [vmem_spec()] * n_head,
        out_specs=vmem_spec(),
        out_shape=jax.ShapeDtypeStruct((n_head * own, wide_cols), BF16),
        scratch_shapes=[pltpu.VMEM((n_head, own, wide_cols), F32)],
        name="order",
    )(me, *row_pieces)
    all_rows = {0: ordered}
    for k in range(2, n_seq, 2):
        all_rows[k] = swap(ordered, "seq", n_seq, k)
    for k in range(0, n_seq, 2):
        all_rows[k + 1] = swap(all_rows[k], "seq", n_seq, 1)
    kl, grad_query_index, grad_head_weight = pl.pallas_call(
        functools.partial(place_kernel, n_seq, heads),
        in_specs=[smem_spec()] + [vmem_spec()] * n_seq,
        out_specs=[vmem_spec()] * 3,
        out_shape=[
            jax.ShapeDtypeStruct((1, rows), BF16),
            jax.ShapeDtypeStruct((rows, heads * width), BF16),
            jax.ShapeDtypeStruct((rows, heads), BF16),
        ],
        scratch_shapes=[pltpu.VMEM((rows, LANES), F32)],
        name="place",
    )(me, *[all_rows[k] for k in range(n_seq)])
    return kl.reshape(rows), grad_query_index, grad_head_weight, grad_key_index


def plain_local(query_mla, key_mla, lse, query_index, key_index, head_weight, query_pos, key_block):
    row_count = query_mla.shape[0]
    key_count = key_mla.shape[0]
    mla_heads = lse.shape[1]
    head_width = query_mla.shape[1] // mla_heads
    index_heads = head_weight.shape[1]
    index_width = key_index.shape[1]
    queries = query_mla.reshape(row_count, mla_heads, head_width)
    mla_keys = key_mla.reshape(key_count, mla_heads, head_width)
    positions = key_block[0] * key_count + jnp.arange(key_count, dtype=jnp.int32)
    valid = positions[None, :] <= query_pos[:, None]
    score = jnp.einsum(
        "thd,jhd->htj", queries, mla_keys, preferred_element_type=jnp.float32
    ) * head_width ** (-0.5)
    attention_part = jnp.sum(
        jnp.where(valid[None], jnp.exp(score - lse.T[:, :, None]), 0.0), axis=0
    )
    indexer_q = query_index.reshape(row_count, index_heads, index_width)
    dots = jnp.einsum("tid,jd->tij", indexer_q, key_index, preferred_element_type=jnp.float32)
    rectified = jnp.maximum(dots, 0.0)
    logit_part = jnp.sum(head_weight[:, :, None] * rectified, axis=1)
    attention, logit = lax.psum((attention_part, logit_part), "head")
    masked = jnp.where(valid, logit, -1e30)
    local_peak = jnp.max(masked, axis=1)
    peak = lax.pmax(local_peak, "seq")
    shifted = jnp.where(valid, jnp.exp(masked - peak[:, None]), 0.0)
    norm, total = lax.psum((jnp.sum(shifted, axis=1), jnp.sum(attention, axis=1)), "seq")
    target = attention / total[:, None]
    log_prob = masked - peak[:, None] - jnp.log(norm)[:, None]
    prob = jnp.where(valid, jnp.exp(log_prob), 0.0)
    log_target = jnp.log(jnp.where(valid, attention, 1.0)) - jnp.log(total)[:, None]
    kl_part = jnp.sum(jnp.where(valid, target * (log_target - log_prob), 0.0), axis=1)
    dlogit = jnp.where(valid, prob - target, 0.0).astype(jnp.bfloat16)
    grad_rows = dlogit.astype(jnp.float32)
    weight_part = jnp.sum(grad_rows[:, None, :] * rectified, axis=2)
    opened = dots > 0
    gated = jnp.where(opened, dlogit[:, None, :], 0)
    query_part = jnp.einsum(
        "tij,jd->tid", gated, key_index, preferred_element_type=jnp.float32
    ).reshape(row_count, index_heads * index_width)
    coef = jnp.where(opened, grad_rows[:, None, :] * head_weight[:, :, None], 0.0).astype(
        jnp.bfloat16
    )
    key_part = jnp.einsum("tij,tid->jd", coef, indexer_q, preferred_element_type=jnp.float32)
    grad_key_index = lax.psum(key_part, "head").astype(jnp.bfloat16)
    query_sum, weight_sum, kl_sum = lax.psum((query_part, weight_part, kl_part), "seq")
    scaled = query_sum.reshape(row_count, index_heads, index_width) * head_weight[:, :, None]
    grad_query_index = scaled.reshape(row_count, index_heads * index_width).astype(jnp.bfloat16)
    grad_head_weight = weight_sum.astype(jnp.bfloat16)
    kl = kl_sum.astype(jnp.bfloat16)
    return (kl, grad_query_index, grad_head_weight, grad_key_index)


def solution(mesh):
    placed = (
        P(None, "head"),
        P("seq", "head"),
        P(None, "head"),
        P(None, "head"),
        P("seq", None),
        P(None, "head"),
        P(),
        P("seq"),
    )
    n_seq, n_head = mesh.shape["seq"], mesh.shape["head"]

    def local(*args):
        rows, heads = args[0].shape[0], args[5].shape[1]
        if rows == 8 * n_seq * n_head and heads % n_seq == 0:
            return fast_local(n_seq, n_head, *args)
        return plain_local(*args)

    return jax.shard_map(
        local,
        mesh=mesh,
        in_specs=placed,
        out_specs=(P(), P(None, "head"), P(None, "head"), P("seq", None)),
        check_vma=False,
    )
```

```python
import functools
import math

import jax
import jax.numpy as jnp
from jax import lax
from jax.experimental import pallas as pl
from jax.experimental.pallas import tpu as pltpu
from jax.sharding import PartitionSpec as P

BF16 = jnp.bfloat16
F32 = jnp.float32
LANES = 128
NT = (((1,), (1,)), ((), ()))


def vmem_spec():
    return pl.BlockSpec(memory_space=pltpu.VMEM)


def smem_spec():
    return pl.BlockSpec(memory_space=pltpu.SMEM)


def head_parts(heads, width):
    least = LANES // math.gcd(LANES, width)
    first = heads // 2 // least * least
    return [first, heads - first] if first > 0 else [heads]


def bits(n):
    return [1 << b for b in range(n.bit_length() - 1)]


def attention_kernel(
    parts, me_ref, block_ref, pos_hbm, q_hbm, k_hbm, lse_hbm, qi_hbm, hw_hbm, out_ref,
    pos_ref, q_ref, k_ref, lse_ref, hw_ref, acc_ref, sems, part_sems
):
    rows, keys = q_ref.shape[0], k_ref.shape[0]
    mla_heads, heads = lse_ref.shape[0], hw_ref.shape[0]
    width = q_ref.shape[1] // mla_heads
    cols = out_ref.shape[1] - keys - LANES
    log2e = math.log2(math.e)
    scale = width ** (-0.5) * log2e
    small = [
        pltpu.make_async_copy(source, target, sems.at[i])
        for i, (source, target) in enumerate(((lse_hbm, lse_ref), (hw_hbm, hw_ref), (pos_hbm, pos_ref)))
    ]
    share_at = pl.ds(pl.multiple_of(me_ref[0] * cols, LANES), cols)
    share_copy = pltpu.make_async_copy(qi_hbm.at[:, share_at], out_ref.at[:, keys : keys + cols], sems.at[3])
    large = []
    first = 0
    for i, n in enumerate(parts):
        at = slice(first * width, (first + n) * width)
        large.append(
            (
                pltpu.make_async_copy(q_hbm.at[:, at], q_ref.at[:, at], part_sems.at[0, i]),
                pltpu.make_async_copy(k_hbm.at[:, at], k_ref.at[:, at], part_sems.at[1, i]),
            )
        )
        first += n
    for copy in large[0]:
        copy.start()
    for copy in small:
        copy.start()
    for pair in large[1:]:
        for copy in pair:
            copy.start()
    share_copy.start()
    for copy in small:
        copy.wait()
    padded = jnp.concatenate([hw_ref[...], jnp.zeros((LANES - heads, rows), F32)], axis=0)
    weight = jnp.transpose(padded)
    high = weight.astype(BF16).astype(F32)
    rest = weight - high
    mid = rest.astype(BF16).astype(F32)
    side = high + pltpu.roll(mid, heads, 1) + pltpu.roll(rest - mid, 2 * heads, 1)
    out_ref[:, keys + cols :] = side.astype(BF16)
    first = 0
    for i, n in enumerate(parts):
        for copy in large[i]:
            copy.wait()
        total = None
        for a in range(first, first + n):
            low, high = a * width, (a + 1) * width
            start, stop = low // LANES * LANES, -(-high // LANES) * LANES
            q = q_ref[:, start:stop]
            if start != low or stop != high:
                at = lax.broadcasted_iota(jnp.int32, (1, stop - start), 1) + start
                q = jnp.where((at >= low) & (at < high), q, jnp.zeros_like(q))
            score = lax.dot_general(k_ref[:, start:stop], q, NT, preferred_element_type=F32)
            value = jnp.exp2(score * scale - lse_ref[a : a + 1, :] * log2e)
            total = value if total is None else total + value
        if first == 0:
            acc_ref[...] = total
        else:
            acc_ref[...] += total
        first += n
    position = block_ref[0] * keys + lax.broadcasted_iota(jnp.int32, (keys, rows), 0)
    share = jnp.where(position <= pos_ref[...], acc_ref[...], -1.0)
    out_ref[:, :keys] = jnp.transpose(share).astype(BF16)
    share_copy.wait()


def keys_kernel(n_seq, n_head, own, me_ref, got_ref, *refs):
    key_refs = refs[:n_seq]
    near_ref, far_ref, gated_ref, q_ref, wide_ref, kl_ref, dots_ref, logit_ref = refs[n_seq:]
    s = me_ref[0]
    keys, width = key_refs[0].shape
    heads_all = wide_ref.shape[0]
    heads = heads_all // n_head
    per = heads // n_seq
    cols = per * width
    group = n_head * own
    for ss in range(n_seq):
        for pair in range(0, n_head, 2):
            at = ss * group + pair * own
            both = got_ref[at : at + 2 * own, keys : keys + cols].astype(F32)
            for e in range(2):
                part = both[e * own : (e + 1) * own]
                tiles = [part[:, i * width : (i + 1) * width] for i in range(per)]
                first = ((pair + e) * heads + ss * per) * own
                q_ref[first : first + per * own, :] = jnp.concatenate(tiles, axis=0).astype(BF16)
    for pair in range(0, n_head, 2):
        both = got_ref[pair * own : (pair + 2) * own, keys + cols :].astype(F32)
        for e in range(2):
            side = both[e * own : (e + 1) * own]
            for i in range(heads):
                one = side[:, i : i + 1] + side[:, heads + i : heads + i + 1] + side[:, 2 * heads + i : 2 * heads + i + 1]
                wide_ref[(pair + e) * heads + i] = jnp.broadcast_to(one, (own, LANES))
    for k in range(n_seq):
        dots = lax.dot_general(q_ref[...], key_refs[k][...], NT, preferred_element_type=F32)
        dots_ref[k] = dots.astype(BF16)
        cube = jnp.maximum(dots, 0.0).reshape(heads_all, own, keys)
        for c in range(0, keys, LANES):
            logit_ref[k, :, c : c + LANES] = jnp.sum(cube[:, :, c : c + LANES] * wide_ref[...], axis=0)
    shares, valids, logits = [], [], []
    peak = jnp.full((own, 1), -1e30, F32)
    for k in range(n_seq):
        src = pl.multiple_of((s ^ k) * group, group)
        cube = got_ref[pl.ds(src, group), :keys].astype(F32).reshape(n_head, own, keys)
        valid = cube[0] >= 0.0
        shares.append(jnp.where(valid, jnp.sum(cube, axis=0), 0.0))
        valids.append(valid)
        logits.append(jnp.where(valid, logit_ref[k], -1e30))
        peak = jnp.maximum(peak, jnp.max(logits[k], axis=1, keepdims=True))

    def row_sum(parts):
        return jnp.sum(sum(parts[1:], parts[0]), axis=1, keepdims=True)

    total = row_sum(shares)
    norm = row_sum([jnp.where(v, jnp.exp(x - peak), 0.0) for v, x in zip(valids, logits)])
    log_norm, log_total, inverse = jnp.log(norm), jnp.log(total), 1.0 / total
    weighted = jnp.transpose(q_ref[...].astype(F32) * wide_ref[...].reshape(q_ref.shape)).astype(BF16)
    kls = []
    for k in range(n_seq):
        target = shares[k] * inverse
        log_prob = logits[k] - peak - log_norm
        prob = jnp.where(valids[k], jnp.exp(log_prob), 0.0)
        log_target = jnp.log(jnp.where(valids[k], shares[k], 1.0)) - log_total
        kls.append(jnp.where(valids[k], target * (log_target - log_prob), 0.0))
        dlogit = jnp.where(valids[k], prob - target, 0.0).astype(BF16).astype(F32)
        cube = dots_ref[k].astype(F32).reshape(heads_all, own, keys)
        gated = jnp.where(cube > 0.0, dlogit[None], 0.0).reshape(heads_all * own, keys).astype(BF16)
        gated_ref[k] = gated
        side = jnp.transpose(jnp.dot(weighted, gated, preferred_element_type=F32))
        if k % 2 == 0:
            near_ref[k // 2] = side
        else:
            far_ref[k // 2] = side.astype(BF16)
    kl_ref[...] = jnp.broadcast_to(row_sum(kls), kl_ref.shape)


def queries_kernel(n_seq, n_head, own, gated_ref, q_ref, wide_ref, kl_ref, *refs):
    key_refs, out_ref = refs[:n_seq], refs[n_seq]
    keys, width = key_refs[0].shape
    heads_all = wide_ref.shape[0]
    heads = heads_all // n_head
    term = None
    for k in range(n_seq):
        part = jnp.dot(gated_ref[k], key_refs[k][...], preferred_element_type=F32)
        term = part if term is None else term + part
    per_head = jnp.sum((term * q_ref[...].astype(F32)).reshape(heads_all, own, width), axis=2, keepdims=True)
    scaled = term.reshape(heads_all, own, width) * wide_ref[...]
    lane = lax.broadcasted_iota(jnp.int32, (own, LANES), 1)
    for pair in range(0, n_head, 2):
        rows = slice(pair * own, (pair + 2) * own)
        one, two = pair * heads, (pair + 1) * heads
        first = second = jnp.where(lane == heads, kl_ref[...], 0.0)
        for i in range(heads):
            both = jnp.concatenate([scaled[one + i], scaled[two + i]], axis=0)
            out_ref[rows, i * width : (i + 1) * width] = both.astype(BF16)
            first = jnp.where(lane == i, per_head[one + i], first)
            second = jnp.where(lane == i, per_head[two + i], second)
        out_ref[rows, heads * width :] = jnp.concatenate([first, second], axis=0).astype(BF16)


def place_kernel(n_seq, me_ref, *refs):
    pieces = refs[:n_seq]
    gq_ref, hw_ref, kl_ref, side_ref, sems = refs[n_seq:]
    s = me_ref[0]
    rows, cols = pieces[0].shape[0], gq_ref.shape[1]
    heads = hw_ref.shape[0]
    copies = []
    for k in range(n_seq):
        at = pl.ds(pl.multiple_of((s ^ k) * rows, rows), rows)
        copies.append(pltpu.make_async_copy(pieces[k].at[:, :cols], gq_ref.at[at, :], sems.at[k]))
        copies[k].start()
        side_ref[at, :] = pieces[k][:, cols:].astype(F32)
    side = jnp.transpose(side_ref[...])
    hw_ref[...] = side[:heads, :].astype(BF16)
    kl_ref[...] = side[heads, :].astype(BF16)
    for copy in copies:
        copy.wait()


def fast_local(n_seq, n_head, query_mla, key_mla, lse, query_index, key_index, head_weight, query_pos, key_block):
    rows, keys = query_mla.shape[0], key_mla.shape[0]
    mla_heads = lse.shape[1]
    mla_width = query_mla.shape[1] // mla_heads
    heads, width = head_weight.shape[1], key_index.shape[1]
    own = rows // (n_seq * n_head)
    group = n_head * own
    heads_all = heads * n_head
    half = n_seq // 2
    wide_cols = heads * width + LANES
    me = jnp.stack([lax.axis_index("seq"), lax.axis_index("head")]).astype(jnp.int32)

    def swap(x, axis, n, mask):
        return lax.ppermute(x, axis, [(i, i ^ mask) for i in range(n)])

    def limit(mib):
        return pltpu.CompilerParams(vmem_limit_bytes=mib * 2**20)

    cols = query_index.shape[1] // n_seq
    parts = head_parts(mla_heads, mla_width)
    hbm = pl.BlockSpec(memory_space=pltpu.HBM)
    sent = pl.pallas_call(
        functools.partial(attention_kernel, parts),
        in_specs=[smem_spec()] * 2 + [hbm] * 6,
        out_specs=vmem_spec(),
        out_shape=jax.ShapeDtypeStruct((rows, keys + cols + LANES), BF16),
        scratch_shapes=[
            pltpu.VMEM((1, rows), jnp.int32),
            pltpu.VMEM(query_mla.shape, BF16),
            pltpu.VMEM(key_mla.shape, BF16),
            pltpu.VMEM((mla_heads, rows), F32),
            pltpu.VMEM((heads, rows), F32),
            pltpu.VMEM((keys, rows), F32),
            pltpu.SemaphoreType.DMA((4,)),
            pltpu.SemaphoreType.DMA((2, len(parts))),
        ],
        compiler_params=limit(56),
        cost_estimate=pl.CostEstimate(
            flops=4 * rows * keys * mla_heads * mla_width,
            bytes_accessed=2 * (rows + keys) * mla_heads * mla_width,
            transcendentals=rows * keys * mla_heads,
        ),
        name="attention",
    )(me, key_block, query_pos.reshape(1, rows), query_mla, key_mla, lse.T, query_index, head_weight.T)

    near_keys = [key_index] + [swap(key_index, "seq", n_seq, k) for k in range(2, n_seq, 2)]
    sent, *near_keys = lax.optimization_barrier((sent, *near_keys))
    got = lax.all_to_all(sent, ("seq", "head"), 0, 0, tiled=True)
    all_keys = []
    for piece in near_keys:
        all_keys += [piece, swap(piece, "seq", n_seq, 1)]

    product = pl.CostEstimate(
        flops=4 * own * heads_all * n_seq * keys * width, bytes_accessed=2**21, transcendentals=0
    )
    near, far, gated, queries, wide, kl_rows = pl.pallas_call(
        functools.partial(keys_kernel, n_seq, n_head, own),
        in_specs=[smem_spec()] + [vmem_spec()] * (1 + n_seq),
        out_specs=[vmem_spec()] * 6,
        out_shape=[
            jax.ShapeDtypeStruct((half, keys, width), F32),
            jax.ShapeDtypeStruct((half, keys, width), BF16),
            jax.ShapeDtypeStruct((n_seq, heads_all * own, keys), BF16),
            jax.ShapeDtypeStruct((heads_all * own, width), BF16),
            jax.ShapeDtypeStruct((heads_all, own, LANES), F32),
            jax.ShapeDtypeStruct((own, LANES), F32),
        ],
        scratch_shapes=[
            pltpu.VMEM((n_seq, heads_all * own, keys), BF16),
            pltpu.VMEM((n_seq, own, keys), F32),
        ],
        compiler_params=limit(20),
        cost_estimate=product,
        name="key_grad",
    )(me, got, *all_keys)

    far = swap(far, "seq", n_seq, 1)
    paired = [near[e] + far[e].astype(F32) for e in range(half)]
    sides = [x.astype(BF16) for x in paired[1:]]
    gated, *sides = lax.optimization_barrier((gated, *sides))
    mine = paired[0]
    for e in range(1, half):
        mine = mine + swap(sides[e - 1], "seq", n_seq, 2 * e).astype(F32)

    rows_out = pl.pallas_call(
        functools.partial(queries_kernel, n_seq, n_head, own),
        in_specs=[vmem_spec()] * (4 + n_seq),
        out_specs=vmem_spec(),
        out_shape=jax.ShapeDtypeStruct((group, wide_cols), BF16),
        compiler_params=limit(16),
        cost_estimate=product,
        name="query_grad",
    )(gated, queries, wide, kl_rows, *all_keys)
    own_rows = lax.all_to_all(rows_out, "head", 0, 0, tiled=True)
    own_rows, _ = lax.optimization_barrier((own_rows, mine))
    steps = bits(n_head)
    for mask in steps[:-1]:
        mine = mine + swap(mine.astype(BF16), "head", n_head, mask).astype(F32)
    last = swap(mine.astype(BF16), "head", n_head, steps[-1])

    all_rows = {0: own_rows}
    for k in range(2, n_seq, 2):
        all_rows[k] = swap(all_rows[0], "seq", n_seq, k)
    for k in range(0, n_seq, 2):
        all_rows[k + 1] = swap(all_rows[k], "seq", n_seq, 1)
    grad_query_index, hw, kl = pl.pallas_call(
        functools.partial(place_kernel, n_seq),
        in_specs=[smem_spec()] + [vmem_spec()] * n_seq,
        out_specs=[pl.BlockSpec(memory_space=pl.ANY), vmem_spec(), vmem_spec()],
        out_shape=[
            jax.ShapeDtypeStruct((rows, heads * width), BF16),
            jax.ShapeDtypeStruct((heads, rows), BF16),
            jax.ShapeDtypeStruct((rows,), BF16),
        ],
        scratch_shapes=[pltpu.VMEM((rows, LANES), F32), pltpu.SemaphoreType.DMA((n_seq,))],
        compiler_params=limit(4),
        cost_estimate=pl.CostEstimate(flops=0, bytes_accessed=8 * rows * wide_cols, transcendentals=0),
        name="place",
    )(me, *[all_rows[k] for k in range(n_seq)])
    grad_key_index = (mine + last.astype(F32)).astype(BF16)
    return kl, grad_query_index, hw.T, grad_key_index


def plain_local(query_mla, key_mla, lse, query_index, key_index, head_weight, query_pos, key_block):
    row_count = query_mla.shape[0]
    key_count = key_mla.shape[0]
    mla_heads = lse.shape[1]
    head_width = query_mla.shape[1] // mla_heads
    index_heads = head_weight.shape[1]
    index_width = key_index.shape[1]
    queries = query_mla.reshape(row_count, mla_heads, head_width)
    mla_keys = key_mla.reshape(key_count, mla_heads, head_width)
    positions = key_block[0] * key_count + jnp.arange(key_count, dtype=jnp.int32)
    valid = positions[None, :] <= query_pos[:, None]
    score = jnp.einsum(
        "thd,jhd->htj", queries, mla_keys, preferred_element_type=jnp.float32
    ) * head_width ** (-0.5)
    attention_part = jnp.sum(
        jnp.where(valid[None], jnp.exp(score - lse.T[:, :, None]), 0.0), axis=0
    )
    indexer_q = query_index.reshape(row_count, index_heads, index_width)
    dots = jnp.einsum("tid,jd->tij", indexer_q, key_index, preferred_element_type=jnp.float32)
    rectified = jnp.maximum(dots, 0.0)
    logit_part = jnp.sum(head_weight[:, :, None] * rectified, axis=1)
    attention, logit = lax.psum((attention_part, logit_part), "head")
    masked = jnp.where(valid, logit, -1e30)
    local_peak = jnp.max(masked, axis=1)
    peak = lax.pmax(local_peak, "seq")
    shifted = jnp.where(valid, jnp.exp(masked - peak[:, None]), 0.0)
    norm, total = lax.psum((jnp.sum(shifted, axis=1), jnp.sum(attention, axis=1)), "seq")
    target = attention / total[:, None]
    log_prob = masked - peak[:, None] - jnp.log(norm)[:, None]
    prob = jnp.where(valid, jnp.exp(log_prob), 0.0)
    log_target = jnp.log(jnp.where(valid, attention, 1.0)) - jnp.log(total)[:, None]
    kl_part = jnp.sum(jnp.where(valid, target * (log_target - log_prob), 0.0), axis=1)
    dlogit = jnp.where(valid, prob - target, 0.0).astype(jnp.bfloat16)
    grad_rows = dlogit.astype(jnp.float32)
    weight_part = jnp.sum(grad_rows[:, None, :] * rectified, axis=2)
    opened = dots > 0
    gated = jnp.where(opened, dlogit[:, None, :], 0)
    query_part = jnp.einsum(
        "tij,jd->tid", gated, key_index, preferred_element_type=jnp.float32
    ).reshape(row_count, index_heads * index_width)
    coef = jnp.where(opened, grad_rows[:, None, :] * head_weight[:, :, None], 0.0).astype(
        jnp.bfloat16
    )
    key_part = jnp.einsum("tij,tid->jd", coef, indexer_q, preferred_element_type=jnp.float32)
    grad_key_index = lax.psum(key_part, "head").astype(jnp.bfloat16)
    query_sum, weight_sum, kl_sum = lax.psum((query_part, weight_part, kl_part), "seq")
    scaled = query_sum.reshape(row_count, index_heads, index_width) * head_weight[:, :, None]
    grad_query_index = scaled.reshape(row_count, index_heads * index_width).astype(jnp.bfloat16)
    grad_head_weight = weight_sum.astype(jnp.bfloat16)
    kl = kl_sum.astype(jnp.bfloat16)
    return (kl, grad_query_index, grad_head_weight, grad_key_index)


def solution(mesh):
    placed = (
        P(None, "head"),
        P("seq", "head"),
        P(None, "head"),
        P(None, "head"),
        P("seq", None),
        P(None, "head"),
        P(),
        P("seq"),
    )
    n_seq, n_head = mesh.shape["seq"], mesh.shape["head"]

    def local(*args):
        rows, heads = args[0].shape[0], args[5].shape[1]
        if rows == 8 * n_seq * n_head and heads % n_seq == 0:
            return fast_local(n_seq, n_head, *args)
        return plain_local(*args)

    return jax.shard_map(
        local,
        mesh=mesh,
        in_specs=placed,
        out_specs=(P(), P(None, "head"), P(None, "head"), P("seq", None)),
        check_vma=False,
    )
```

```python
import functools
import math

import jax
import jax.numpy as jnp
from jax import lax
from jax.experimental import pallas as pl
from jax.experimental.pallas import tpu as pltpu
from jax.sharding import PartitionSpec as P

BF16 = jnp.bfloat16
F32 = jnp.float32
LANES = 128
NT = (((1,), (1,)), ((), ()))


def vmem_spec():
    return pl.BlockSpec(memory_space=pltpu.VMEM)


def smem_spec():
    return pl.BlockSpec(memory_space=pltpu.SMEM)


def head_parts(heads, width):
    least = LANES // math.gcd(LANES, width)
    first = heads // 2 // least * least
    return [first, heads - first] if first > 0 else [heads]


def bits(n):
    return [1 << b for b in range(n.bit_length() - 1)]


def attention_kernel(
    parts, block_ref, pos_hbm, q_hbm, k_hbm, lse_hbm, qi_hbm, hw_hbm, out_ref,
    pos_ref, q_ref, k_ref, lse_ref, hw_ref, acc_ref, sems, part_sems
):
    rows, keys = q_ref.shape[0], k_ref.shape[0]
    mla_heads, heads = lse_ref.shape[0], hw_ref.shape[0]
    width = q_ref.shape[1] // mla_heads
    cols = out_ref.shape[1] - keys - LANES
    log2e = math.log2(math.e)
    scale = width ** (-0.5) * log2e
    small = [
        pltpu.make_async_copy(source, target, sems.at[i])
        for i, (source, target) in enumerate(((lse_hbm, lse_ref), (hw_hbm, hw_ref), (pos_hbm, pos_ref)))
    ]
    share_at = pl.ds(pl.multiple_of(lax.axis_index("seq") * cols, LANES), cols)
    share_copy = pltpu.make_async_copy(qi_hbm.at[:, share_at], out_ref.at[:, keys : keys + cols], sems.at[3])
    large = []
    first = 0
    for i, n in enumerate(parts):
        at = slice(first * width, (first + n) * width)
        large.append(
            (
                pltpu.make_async_copy(q_hbm.at[:, at], q_ref.at[:, at], part_sems.at[0, i]),
                pltpu.make_async_copy(k_hbm.at[:, at], k_ref.at[:, at], part_sems.at[1, i]),
            )
        )
        first += n
    for copy in large[0]:
        copy.start()
    for copy in small:
        copy.start()
    for pair in large[1:]:
        for copy in pair:
            copy.start()
    share_copy.start()
    for copy in small:
        copy.wait()
    padded = jnp.concatenate([hw_ref[...], jnp.zeros((LANES - heads, rows), F32)], axis=0)
    weight = jnp.transpose(padded)
    high = weight.astype(BF16).astype(F32)
    rest = weight - high
    mid = rest.astype(BF16).astype(F32)
    side = high + pltpu.roll(mid, heads, 1) + pltpu.roll(rest - mid, 2 * heads, 1)
    out_ref[:, keys + cols :] = side.astype(BF16)
    first = 0
    for i, n in enumerate(parts):
        for copy in large[i]:
            copy.wait()
        total = None
        for a in range(first, first + n):
            low, high = a * width, (a + 1) * width
            start, stop = low // LANES * LANES, -(-high // LANES) * LANES
            q = q_ref[:, start:stop]
            if start != low or stop != high:
                at = lax.broadcasted_iota(jnp.int32, (1, stop - start), 1) + start
                q = jnp.where((at >= low) & (at < high), q, jnp.zeros_like(q))
            score = lax.dot_general(k_ref[:, start:stop], q, NT, preferred_element_type=F32)
            value = jnp.exp2(score * scale - lse_ref[a : a + 1, :] * log2e)
            total = value if total is None else total + value
        if first == 0:
            acc_ref[...] = total
        else:
            acc_ref[...] += total
        first += n
    position = block_ref[0] * keys + lax.broadcasted_iota(jnp.int32, (keys, rows), 0)
    share = jnp.where(position <= pos_ref[...], acc_ref[...], -1.0)
    out_ref[:, :keys] = jnp.transpose(share).astype(BF16)
    share_copy.wait()


def keys_kernel(n_seq, n_head, own, got_ref, *refs):
    key_refs = refs[:n_seq]
    far_ref, gated_ref, q_ref, wide_ref, kl_ref, weighted_ref, dots_ref, logit_ref = refs[n_seq:]
    s = lax.axis_index("seq")
    keys, width = key_refs[0].shape
    heads_all = wide_ref.shape[0]
    heads = heads_all // n_head
    per = heads // n_seq
    cols = per * width
    group = n_head * own
    for ss in range(n_seq):
        for pair in range(0, n_head, 2):
            at = ss * group + pair * own
            both = got_ref[at : at + 2 * own, keys : keys + cols].astype(F32)
            for e in range(2):
                part = both[e * own : (e + 1) * own]
                tiles = [part[:, i * width : (i + 1) * width] for i in range(per)]
                first = ((pair + e) * heads + ss * per) * own
                q_ref[first : first + per * own, :] = jnp.concatenate(tiles, axis=0).astype(BF16)
    for pair in range(0, n_head, 2):
        both = got_ref[pair * own : (pair + 2) * own, keys + cols :].astype(F32)
        for e in range(2):
            side = both[e * own : (e + 1) * own]
            for i in range(heads):
                one = side[:, i : i + 1] + side[:, heads + i : heads + i + 1] + side[:, 2 * heads + i : 2 * heads + i + 1]
                wide_ref[(pair + e) * heads + i] = jnp.broadcast_to(one, (own, LANES))
    for k in range(n_seq):
        dots = lax.dot_general(q_ref[...], key_refs[k][...], NT, preferred_element_type=F32)
        dots_ref[k] = dots.astype(BF16)
        cube = jnp.maximum(dots, 0.0).reshape(heads_all, own, keys)
        for c in range(0, keys, LANES):
            logit_ref[k, :, c : c + LANES] = jnp.sum(cube[:, :, c : c + LANES] * wide_ref[...], axis=0)
    shares, valids, logits = [], [], []
    peak = jnp.full((own, 1), -1e30, F32)
    for k in range(n_seq):
        src = pl.multiple_of((s ^ k) * group, group)
        cube = got_ref[pl.ds(src, group), :keys].astype(F32).reshape(n_head, own, keys)
        valid = cube[0] >= 0.0
        shares.append(jnp.where(valid, jnp.sum(cube, axis=0), 0.0))
        valids.append(valid)
        logits.append(jnp.where(valid, logit_ref[k], -1e30))
        peak = jnp.maximum(peak, jnp.max(logits[k], axis=1, keepdims=True))

    def row_sum(parts):
        return jnp.sum(sum(parts[1:], parts[0]), axis=1, keepdims=True)

    total = row_sum(shares)
    norm = row_sum([jnp.where(v, jnp.exp(x - peak), 0.0) for v, x in zip(valids, logits)])
    log_norm, log_total, inverse = jnp.log(norm), jnp.log(total), 1.0 / total
    weighted = jnp.transpose(q_ref[...].astype(F32) * wide_ref[...].reshape(q_ref.shape)).astype(BF16)
    weighted_ref[...] = weighted
    kls = []
    for k in range(n_seq):
        target = shares[k] * inverse
        log_prob = logits[k] - peak - log_norm
        prob = jnp.where(valids[k], jnp.exp(log_prob), 0.0)
        log_target = jnp.log(jnp.where(valids[k], shares[k], 1.0)) - log_total
        kls.append(jnp.where(valids[k], target * (log_target - log_prob), 0.0))
        dlogit = jnp.where(valids[k], prob - target, 0.0).astype(BF16).astype(F32)
        cube = dots_ref[k].astype(F32).reshape(heads_all, own, keys)
        gated = jnp.where(cube > 0.0, dlogit[None], 0.0).reshape(heads_all * own, keys).astype(BF16)
        gated_ref[k] = gated
        if k % 2 == 1:
            side = jnp.dot(weighted, gated, preferred_element_type=F32)
            far_ref[k // 2] = jnp.transpose(side).astype(BF16)
    kl_ref[...] = jnp.broadcast_to(row_sum(kls), kl_ref.shape)


def products_kernel(n_seq, gated_ref, weighted_ref, *refs):
    key_refs, near_ref, term_ref = refs[:n_seq], refs[n_seq], refs[n_seq + 1]
    term = None
    for k in range(n_seq):
        if k % 2 == 0:
            side = jnp.dot(weighted_ref[...], gated_ref[k], preferred_element_type=F32)
            near_ref[k // 2] = jnp.transpose(side)
        part = jnp.dot(gated_ref[k], key_refs[k][...], preferred_element_type=F32)
        term = part if term is None else term + part
    term_ref[...] = term


def queries_kernel(n_head, own, term_ref, q_ref, wide_ref, kl_ref, out_ref):
    width = q_ref.shape[1]
    heads_all = wide_ref.shape[0]
    heads = heads_all // n_head
    term = term_ref[...]
    per_head = jnp.sum((term * q_ref[...].astype(F32)).reshape(heads_all, own, width), axis=2, keepdims=True)
    scaled = term.reshape(heads_all, own, width) * wide_ref[...]
    lane = lax.broadcasted_iota(jnp.int32, (own, LANES), 1)
    for pair in range(0, n_head, 2):
        rows = slice(pair * own, (pair + 2) * own)
        one, two = pair * heads, (pair + 1) * heads
        first = second = jnp.where(lane == heads, kl_ref[...], 0.0)
        for i in range(heads):
            both = jnp.concatenate([scaled[one + i], scaled[two + i]], axis=0)
            out_ref[rows, i * width : (i + 1) * width] = both.astype(BF16)
            first = jnp.where(lane == i, per_head[one + i], first)
            second = jnp.where(lane == i, per_head[two + i], second)
        out_ref[rows, heads * width :] = jnp.concatenate([first, second], axis=0).astype(BF16)


def place_kernel(n_seq, *refs):
    pieces = refs[:n_seq]
    gq_ref, hw_ref, kl_ref, side_ref, sems = refs[n_seq:]
    s = lax.axis_index("seq")
    rows, cols = pieces[0].shape[0], gq_ref.shape[1]
    heads = hw_ref.shape[0]
    copies = []
    for k in range(n_seq):
        at = pl.ds(pl.multiple_of((s ^ k) * rows, rows), rows)
        copies.append(pltpu.make_async_copy(pieces[k].at[:, :cols], gq_ref.at[at, :], sems.at[k]))
        copies[k].start()
        side_ref[at, :] = pieces[k][:, cols:].astype(F32)
    side = jnp.transpose(side_ref[...])
    hw_ref[...] = side[:heads, :].astype(BF16)
    kl_ref[...] = side[heads, :].astype(BF16)
    for copy in copies:
        copy.wait()


def fast_local(n_seq, n_head, query_mla, key_mla, lse, query_index, key_index, head_weight, query_pos, key_block):
    rows, keys = query_mla.shape[0], key_mla.shape[0]
    mla_heads = lse.shape[1]
    mla_width = query_mla.shape[1] // mla_heads
    heads, width = head_weight.shape[1], key_index.shape[1]
    own = rows // (n_seq * n_head)
    group = n_head * own
    heads_all = heads * n_head
    half = n_seq // 2
    wide_cols = heads * width + LANES

    def swap(x, axis, n, mask):
        return lax.ppermute(x, axis, [(i, i ^ mask) for i in range(n)])

    def limit(mib):
        return pltpu.CompilerParams(vmem_limit_bytes=mib * 2**20)

    cols = query_index.shape[1] // n_seq
    parts = head_parts(mla_heads, mla_width)
    hbm = pl.BlockSpec(memory_space=pltpu.HBM)
    sent = pl.pallas_call(
        functools.partial(attention_kernel, parts),
        in_specs=[smem_spec()] + [hbm] * 6,
        out_specs=vmem_spec(),
        out_shape=jax.ShapeDtypeStruct((rows, keys + cols + LANES), BF16),
        scratch_shapes=[
            pltpu.VMEM((1, rows), jnp.int32),
            pltpu.VMEM(query_mla.shape, BF16),
            pltpu.VMEM(key_mla.shape, BF16),
            pltpu.VMEM((mla_heads, rows), F32),
            pltpu.VMEM((heads, rows), F32),
            pltpu.VMEM((keys, rows), F32),
            pltpu.SemaphoreType.DMA((4,)),
            pltpu.SemaphoreType.DMA((2, len(parts))),
        ],
        compiler_params=limit(56),
        cost_estimate=pl.CostEstimate(
            flops=4 * rows * keys * mla_heads * mla_width,
            bytes_accessed=2 * (rows + keys) * mla_heads * mla_width,
            transcendentals=rows * keys * mla_heads,
        ),
        name="attention",
    )(key_block, query_pos.reshape(1, rows), query_mla, key_mla, lse.T, query_index, head_weight.T)

    near_keys = [key_index] + [swap(key_index, "seq", n_seq, k) for k in range(2, n_seq, 2)]
    sent, *held = lax.optimization_barrier((sent, *near_keys[:-1]))
    near_keys = held + near_keys[-1:]
    got = lax.all_to_all(sent, ("seq", "head"), 0, 0, tiled=True)
    all_keys = []
    for piece in near_keys:
        all_keys += [piece, swap(piece, "seq", n_seq, 1)]

    product = pl.CostEstimate(
        flops=4 * own * heads_all * n_seq * keys * width, bytes_accessed=2**21, transcendentals=0
    )
    far, gated, queries, wide, kl_rows, weighted = pl.pallas_call(
        functools.partial(keys_kernel, n_seq, n_head, own),
        in_specs=[vmem_spec()] * (1 + n_seq),
        out_specs=[vmem_spec()] * 6,
        out_shape=[
            jax.ShapeDtypeStruct((half, keys, width), BF16),
            jax.ShapeDtypeStruct((n_seq, heads_all * own, keys), BF16),
            jax.ShapeDtypeStruct((heads_all * own, width), BF16),
            jax.ShapeDtypeStruct((heads_all, own, LANES), F32),
            jax.ShapeDtypeStruct((own, LANES), F32),
            jax.ShapeDtypeStruct((width, heads_all * own), BF16),
        ],
        scratch_shapes=[
            pltpu.VMEM((n_seq, heads_all * own, keys), BF16),
            pltpu.VMEM((n_seq, own, keys), F32),
        ],
        compiler_params=limit(20),
        cost_estimate=product,
        name="key_grad",
    )(got, *all_keys)

    far = swap(far, "seq", n_seq, 1)
    near, term = pl.pallas_call(
        functools.partial(products_kernel, n_seq),
        in_specs=[vmem_spec()] * (2 + n_seq),
        out_specs=[vmem_spec()] * 2,
        out_shape=[
            jax.ShapeDtypeStruct((half, keys, width), F32),
            jax.ShapeDtypeStruct((heads_all * own, width), F32),
        ],
        compiler_params=limit(16),
        cost_estimate=product,
        name="products",
    )(gated, weighted, *all_keys)
    paired = [near[e] + far[e].astype(F32) for e in range(half)]
    sides = [x.astype(BF16) for x in paired[1:]]
    term, *sides = lax.optimization_barrier((term, *sides))
    mine = paired[0]
    for e in range(1, half):
        mine = mine + swap(sides[e - 1], "seq", n_seq, 2 * e).astype(F32)

    rows_out = pl.pallas_call(
        functools.partial(queries_kernel, n_head, own),
        in_specs=[vmem_spec()] * 4,
        out_specs=vmem_spec(),
        out_shape=jax.ShapeDtypeStruct((group, wide_cols), BF16),
        compiler_params=limit(16),
        cost_estimate=pl.CostEstimate(flops=0, bytes_accessed=2**21, transcendentals=0),
        name="query_grad",
    )(term, queries, wide, kl_rows)
    own_rows = lax.all_to_all(rows_out, "head", 0, 0, tiled=True)
    own_rows, _ = lax.optimization_barrier((own_rows, mine))
    steps = bits(n_head)
    for mask in steps[:-1]:
        mine = mine + swap(mine.astype(BF16), "head", n_head, mask).astype(F32)
    last = swap(mine.astype(BF16), "head", n_head, steps[-1])

    all_rows = {0: own_rows}
    for k in range(2, n_seq, 2):
        all_rows[k] = swap(all_rows[0], "seq", n_seq, k)
    for k in range(0, n_seq, 2):
        all_rows[k + 1] = swap(all_rows[k], "seq", n_seq, 1)
    grad_query_index, hw, kl = pl.pallas_call(
        functools.partial(place_kernel, n_seq),
        in_specs=[vmem_spec()] * n_seq,
        out_specs=[pl.BlockSpec(memory_space=pl.ANY), vmem_spec(), vmem_spec()],
        out_shape=[
            jax.ShapeDtypeStruct((rows, heads * width), BF16),
            jax.ShapeDtypeStruct((heads, rows), BF16),
            jax.ShapeDtypeStruct((rows,), BF16),
        ],
        scratch_shapes=[pltpu.VMEM((rows, LANES), F32), pltpu.SemaphoreType.DMA((n_seq,))],
        compiler_params=limit(4),
        cost_estimate=pl.CostEstimate(flops=0, bytes_accessed=8 * rows * wide_cols, transcendentals=0),
        name="place",
    )(*[all_rows[k] for k in range(n_seq)])
    grad_key_index = (mine + last.astype(F32)).astype(BF16)
    return kl, grad_query_index, hw.T, grad_key_index


def plain_local(query_mla, key_mla, lse, query_index, key_index, head_weight, query_pos, key_block):
    row_count = query_mla.shape[0]
    key_count = key_mla.shape[0]
    mla_heads = lse.shape[1]
    head_width = query_mla.shape[1] // mla_heads
    index_heads = head_weight.shape[1]
    index_width = key_index.shape[1]
    queries = query_mla.reshape(row_count, mla_heads, head_width)
    mla_keys = key_mla.reshape(key_count, mla_heads, head_width)
    positions = key_block[0] * key_count + jnp.arange(key_count, dtype=jnp.int32)
    valid = positions[None, :] <= query_pos[:, None]
    score = jnp.einsum(
        "thd,jhd->htj", queries, mla_keys, preferred_element_type=jnp.float32
    ) * head_width ** (-0.5)
    attention_part = jnp.sum(
        jnp.where(valid[None], jnp.exp(score - lse.T[:, :, None]), 0.0), axis=0
    )
    indexer_q = query_index.reshape(row_count, index_heads, index_width)
    dots = jnp.einsum("tid,jd->tij", indexer_q, key_index, preferred_element_type=jnp.float32)
    rectified = jnp.maximum(dots, 0.0)
    logit_part = jnp.sum(head_weight[:, :, None] * rectified, axis=1)
    attention, logit = lax.psum((attention_part, logit_part), "head")
    masked = jnp.where(valid, logit, -1e30)
    local_peak = jnp.max(masked, axis=1)
    peak = lax.pmax(local_peak, "seq")
    shifted = jnp.where(valid, jnp.exp(masked - peak[:, None]), 0.0)
    norm, total = lax.psum((jnp.sum(shifted, axis=1), jnp.sum(attention, axis=1)), "seq")
    target = attention / total[:, None]
    log_prob = masked - peak[:, None] - jnp.log(norm)[:, None]
    prob = jnp.where(valid, jnp.exp(log_prob), 0.0)
    log_target = jnp.log(jnp.where(valid, attention, 1.0)) - jnp.log(total)[:, None]
    kl_part = jnp.sum(jnp.where(valid, target * (log_target - log_prob), 0.0), axis=1)
    dlogit = jnp.where(valid, prob - target, 0.0).astype(jnp.bfloat16)
    grad_rows = dlogit.astype(jnp.float32)
    weight_part = jnp.sum(grad_rows[:, None, :] * rectified, axis=2)
    opened = dots > 0
    gated = jnp.where(opened, dlogit[:, None, :], 0)
    query_part = jnp.einsum(
        "tij,jd->tid", gated, key_index, preferred_element_type=jnp.float32
    ).reshape(row_count, index_heads * index_width)
    coef = jnp.where(opened, grad_rows[:, None, :] * head_weight[:, :, None], 0.0).astype(
        jnp.bfloat16
    )
    key_part = jnp.einsum("tij,tid->jd", coef, indexer_q, preferred_element_type=jnp.float32)
    grad_key_index = lax.psum(key_part, "head").astype(jnp.bfloat16)
    query_sum, weight_sum, kl_sum = lax.psum((query_part, weight_part, kl_part), "seq")
    scaled = query_sum.reshape(row_count, index_heads, index_width) * head_weight[:, :, None]
    grad_query_index = scaled.reshape(row_count, index_heads * index_width).astype(jnp.bfloat16)
    grad_head_weight = weight_sum.astype(jnp.bfloat16)
    kl = kl_sum.astype(jnp.bfloat16)
    return (kl, grad_query_index, grad_head_weight, grad_key_index)


def solution(mesh):
    placed = (
        P(None, "head"),
        P("seq", "head"),
        P(None, "head"),
        P(None, "head"),
        P("seq", None),
        P(None, "head"),
        P(),
        P("seq"),
    )
    n_seq, n_head = mesh.shape["seq"], mesh.shape["head"]

    def local(*args):
        rows, heads = args[0].shape[0], args[5].shape[1]
        if rows == 8 * n_seq * n_head and heads % n_seq == 0:
            return fast_local(n_seq, n_head, *args)
        return plain_local(*args)

    return jax.shard_map(
        local,
        mesh=mesh,
        in_specs=placed,
        out_specs=(P(), P(None, "head"), P(None, "head"), P("seq", None)),
        check_vma=False,
    )
```

```python
import functools
import math

import jax
import jax.numpy as jnp
from jax import lax
from jax.experimental import pallas as pl
from jax.experimental.pallas import tpu as pltpu
from jax.sharding import PartitionSpec as P

BF16 = jnp.bfloat16
F32 = jnp.float32
LANES = 128
NT = (((1,), (1,)), ((), ()))


def vmem_spec():
    return pl.BlockSpec(memory_space=pltpu.VMEM)


def head_parts(heads, width):
    least = LANES // math.gcd(LANES, width)
    first = heads // 2 // least * least
    return [first, heads - first] if first > 0 else [heads]


def bits(n):
    return [1 << b for b in range(n.bit_length() - 1)]


def attention_kernel(
    parts, block_hbm, pos_hbm, q_hbm, k_hbm, lse_hbm, qi_hbm, hw_hbm, out_ref,
    block_ref, pos_ref, q_ref, k_ref, lse_ref, hw_ref, acc_ref, sems, part_sems
):
    rows, keys = q_ref.shape[0], k_ref.shape[0]
    mla_heads, heads = lse_ref.shape[0], hw_ref.shape[0]
    width = q_ref.shape[1] // mla_heads
    cols = out_ref.shape[1] - keys - LANES
    log2e = math.log2(math.e)
    scale = width ** (-0.5) * log2e
    small = [
        pltpu.make_async_copy(source, target, sems.at[i])
        for i, (source, target) in enumerate(((lse_hbm, lse_ref), (hw_hbm, hw_ref), (pos_hbm, pos_ref), (block_hbm, block_ref)))
    ]
    share_at = pl.ds(pl.multiple_of(lax.axis_index("seq") * cols, LANES), cols)
    share_copy = pltpu.make_async_copy(qi_hbm.at[:, share_at], out_ref.at[:, keys : keys + cols], sems.at[4])
    large = []
    first = 0
    for i, n in enumerate(parts):
        at = slice(first * width, (first + n) * width)
        large.append(
            (
                pltpu.make_async_copy(q_hbm.at[:, at], q_ref.at[:, at], part_sems.at[0, i]),
                pltpu.make_async_copy(k_hbm.at[:, at], k_ref.at[:, at], part_sems.at[1, i]),
            )
        )
        first += n
    for copy in large[0]:
        copy.start()
    for copy in small:
        copy.start()
    for pair in large[1:]:
        for copy in pair:
            copy.start()
    share_copy.start()
    for copy in small:
        copy.wait()
    padded = jnp.concatenate([hw_ref[...], jnp.zeros((LANES - heads, rows), F32)], axis=0)
    weight = jnp.transpose(padded)
    high = weight.astype(BF16).astype(F32)
    rest = weight - high
    mid = rest.astype(BF16).astype(F32)
    side = high + pltpu.roll(mid, heads, 1) + pltpu.roll(rest - mid, 2 * heads, 1)
    out_ref[:, keys + cols :] = side.astype(BF16)
    first = 0
    for i, n in enumerate(parts):
        for copy in large[i]:
            copy.wait()
        total = None
        for a in range(first, first + n):
            low, high = a * width, (a + 1) * width
            start, stop = low // LANES * LANES, -(-high // LANES) * LANES
            q = q_ref[:, start:stop]
            if start != low or stop != high:
                at = lax.broadcasted_iota(jnp.int32, (1, stop - start), 1) + start
                q = jnp.where((at >= low) & (at < high), q, jnp.zeros_like(q))
            score = lax.dot_general(k_ref[:, start:stop], q, NT, preferred_element_type=F32)
            value = jnp.exp2(score * scale - lse_ref[a : a + 1, :] * log2e)
            total = value if total is None else total + value
        if first == 0:
            acc_ref[...] = total
        else:
            acc_ref[...] += total
        first += n
    position = block_ref[0] * keys + lax.broadcasted_iota(jnp.int32, (keys, rows), 0)
    share = jnp.where(position <= pos_ref[...], acc_ref[...], -1.0)
    out_ref[:, :keys] = jnp.transpose(share).astype(BF16)
    share_copy.wait()


def keys_kernel(n_seq, n_head, own, got_ref, *refs):
    key_refs = refs[:n_seq]
    far_ref, gated_ref, q_ref, wide_ref, kl_ref, weighted_ref, dots_ref, logit_ref = refs[n_seq:]
    s = lax.axis_index("seq")
    keys, width = key_refs[0].shape
    heads_all = wide_ref.shape[0]
    heads = heads_all // n_head
    per = heads // n_seq
    cols = per * width
    group = n_head * own
    for ss in range(n_seq):
        for pair in range(0, n_head, 2):
            at = ss * group + pair * own
            both = got_ref[at : at + 2 * own, keys : keys + cols].astype(F32)
            for e in range(2):
                part = both[e * own : (e + 1) * own]
                tiles = [part[:, i * width : (i + 1) * width] for i in range(per)]
                first = ((pair + e) * heads + ss * per) * own
                q_ref[first : first + per * own, :] = jnp.concatenate(tiles, axis=0).astype(BF16)
    for pair in range(0, n_head, 2):
        both = got_ref[pair * own : (pair + 2) * own, keys + cols :].astype(F32)
        for e in range(2):
            side = both[e * own : (e + 1) * own]
            for i in range(heads):
                one = side[:, i : i + 1] + side[:, heads + i : heads + i + 1] + side[:, 2 * heads + i : 2 * heads + i + 1]
                wide_ref[(pair + e) * heads + i] = jnp.broadcast_to(one, (own, LANES))
    for k in range(n_seq):
        dots = lax.dot_general(q_ref[...], key_refs[k][...], NT, preferred_element_type=F32)
        dots_ref[k] = dots.astype(BF16)
        cube = jnp.maximum(dots, 0.0).reshape(heads_all, own, keys)
        for c in range(0, keys, LANES):
            logit_ref[k, :, c : c + LANES] = jnp.sum(cube[:, :, c : c + LANES] * wide_ref[...], axis=0)
    shares, valids, logits = [], [], []
    peak = jnp.full((own, 1), -1e30, F32)
    for k in range(n_seq):
        src = pl.multiple_of((s ^ k) * group, group)
        cube = got_ref[pl.ds(src, group), :keys].astype(F32).reshape(n_head, own, keys)
        valid = cube[0] >= 0.0
        shares.append(jnp.where(valid, jnp.sum(cube, axis=0), 0.0))
        valids.append(valid)
        logits.append(jnp.where(valid, logit_ref[k], -1e30))
        peak = jnp.maximum(peak, jnp.max(logits[k], axis=1, keepdims=True))

    def row_sum(parts):
        return jnp.sum(sum(parts[1:], parts[0]), axis=1, keepdims=True)

    total = row_sum(shares)
    norm = row_sum([jnp.where(v, jnp.exp(x - peak), 0.0) for v, x in zip(valids, logits)])
    log_norm, log_total = jnp.log(norm), jnp.log(total)
    weighted = jnp.transpose(q_ref[...].astype(F32) * wide_ref[...].reshape(q_ref.shape)).astype(BF16)
    weighted_ref[...] = weighted
    kls = []
    for k in range(n_seq):
        target = shares[k] / total
        log_prob = logits[k] - peak - log_norm
        prob = jnp.where(valids[k], jnp.exp(log_prob), 0.0)
        log_target = jnp.log(jnp.where(valids[k], shares[k], 1.0)) - log_total
        kls.append(jnp.where(valids[k], target * (log_target - log_prob), 0.0))
        dlogit = jnp.where(valids[k], prob - target, 0.0)
        twice = jnp.concatenate([dlogit, dlogit], axis=0).astype(BF16)
        cube = dots_ref[k].reshape(heads_all // 2, 2 * own, keys)
        gated = jnp.where(cube > 0, twice[None], jnp.zeros_like(twice)[None]).reshape(heads_all * own, keys)
        gated_ref[k] = gated
        if k % 2 == 1:
            side = jnp.dot(weighted, gated, preferred_element_type=F32)
            far_ref[k // 2] = jnp.transpose(side).astype(BF16)
    kl_ref[...] = jnp.broadcast_to(row_sum(kls), kl_ref.shape)


def products_kernel(n_seq, gated_ref, weighted_ref, *refs):
    key_refs, near_ref, term_ref = refs[:n_seq], refs[n_seq], refs[n_seq + 1]
    term = None
    for k in range(n_seq):
        if k % 2 == 0:
            side = jnp.dot(weighted_ref[...], gated_ref[k], preferred_element_type=F32)
            near_ref[k // 2] = jnp.transpose(side)
        part = jnp.dot(gated_ref[k], key_refs[k][...], preferred_element_type=F32)
        term = part if term is None else term + part
    term_ref[...] = term


def queries_kernel(n_head, own, term_ref, q_ref, wide_ref, kl_ref, out_ref):
    width = q_ref.shape[1]
    heads_all = wide_ref.shape[0]
    heads = heads_all // n_head
    term = term_ref[...]
    per_head = jnp.sum((term * q_ref[...].astype(F32)).reshape(heads_all, own, width), axis=2, keepdims=True)
    scaled = term.reshape(heads_all, own, width) * wide_ref[...]
    lane = lax.broadcasted_iota(jnp.int32, (own, LANES), 1)
    for pair in range(0, n_head, 2):
        rows = slice(pair * own, (pair + 2) * own)
        one, two = pair * heads, (pair + 1) * heads
        first = second = jnp.where(lane == heads, kl_ref[...], 0.0)
        for i in range(heads):
            both = jnp.concatenate([scaled[one + i], scaled[two + i]], axis=0)
            out_ref[rows, i * width : (i + 1) * width] = both.astype(BF16)
            first = jnp.where(lane == i, per_head[one + i], first)
            second = jnp.where(lane == i, per_head[two + i], second)
        out_ref[rows, heads * width :] = jnp.concatenate([first, second], axis=0).astype(BF16)


def place_kernel(n_seq, *refs):
    pieces = refs[:n_seq]
    gq_ref, hw_out, kl_out, side_ref, hw_ref, kl_ref, sems = refs[n_seq:]
    s = lax.axis_index("seq")
    rows, cols = pieces[0].shape[0], gq_ref.shape[1]
    heads = hw_ref.shape[0]
    copies = []
    for k in range(n_seq):
        at = pl.ds(pl.multiple_of((s ^ k) * rows, rows), rows)
        copies.append(pltpu.make_async_copy(pieces[k].at[:, :cols], gq_ref.at[at, :], sems.at[k]))
        copies[k].start()
        side_ref[at, :] = pieces[k][:, cols:].astype(F32)
    side = jnp.transpose(side_ref[...])
    hw_ref[...] = side[:heads, :].astype(BF16)
    kl_ref[...] = side[heads, :].astype(BF16)
    for source, target in ((hw_ref, hw_out), (kl_ref, kl_out)):
        copies.append(pltpu.make_async_copy(source, target, sems.at[len(copies)]))
        copies[-1].start()
    for copy in copies:
        copy.wait()


def fast_local(n_seq, n_head, query_mla, key_mla, lse, query_index, key_index, head_weight, query_pos, key_block):
    rows, keys = query_mla.shape[0], key_mla.shape[0]
    mla_heads = lse.shape[1]
    mla_width = query_mla.shape[1] // mla_heads
    heads, width = head_weight.shape[1], key_index.shape[1]
    own = rows // (n_seq * n_head)
    group = n_head * own
    heads_all = heads * n_head
    half = n_seq // 2
    wide_cols = heads * width + LANES

    def swap(x, axis, n, mask):
        return lax.ppermute(x, axis, [(i, i ^ mask) for i in range(n)])

    def limit(mib):
        return pltpu.CompilerParams(vmem_limit_bytes=mib * 2**20)

    cols = query_index.shape[1] // n_seq
    parts = head_parts(mla_heads, mla_width)
    hbm = pl.BlockSpec(memory_space=pltpu.HBM)
    sent = pl.pallas_call(
        functools.partial(attention_kernel, parts),
        in_specs=[hbm] * 7,
        out_specs=vmem_spec(),
        out_shape=jax.ShapeDtypeStruct((rows, keys + cols + LANES), BF16),
        scratch_shapes=[
            pltpu.SMEM((1,), jnp.int32),
            pltpu.VMEM((1, rows), jnp.int32),
            pltpu.VMEM(query_mla.shape, BF16),
            pltpu.VMEM(key_mla.shape, BF16),
            pltpu.VMEM((mla_heads, rows), F32),
            pltpu.VMEM((heads, rows), F32),
            pltpu.VMEM((keys, rows), F32),
            pltpu.SemaphoreType.DMA((5,)),
            pltpu.SemaphoreType.DMA((2, len(parts))),
        ],
        compiler_params=limit(56),
        cost_estimate=pl.CostEstimate(
            flops=4 * rows * keys * mla_heads * mla_width,
            bytes_accessed=2 * (rows + keys) * mla_heads * mla_width,
            transcendentals=rows * keys * mla_heads,
        ),
        name="attention",
    )(key_block, query_pos.reshape(1, rows), query_mla, key_mla, lse.T, query_index, head_weight.T)

    near_keys = [key_index] + [swap(key_index, "seq", n_seq, k) for k in range(2, n_seq, 2)]
    sent, *held = lax.optimization_barrier((sent, *near_keys[:-1]))
    near_keys = held + near_keys[-1:]
    got = lax.all_to_all(sent, ("seq", "head"), 0, 0, tiled=True)
    all_keys = []
    for piece in near_keys:
        all_keys += [piece, swap(piece, "seq", n_seq, 1)]

    product = pl.CostEstimate(
        flops=4 * own * heads_all * n_seq * keys * width, bytes_accessed=2**21, transcendentals=0
    )
    far, gated, queries, wide, kl_rows, weighted = pl.pallas_call(
        functools.partial(keys_kernel, n_seq, n_head, own),
        in_specs=[vmem_spec()] * (1 + n_seq),
        out_specs=[vmem_spec()] * 6,
        out_shape=[
            jax.ShapeDtypeStruct((half, keys, width), BF16),
            jax.ShapeDtypeStruct((n_seq, heads_all * own, keys), BF16),
            jax.ShapeDtypeStruct((heads_all * own, width), BF16),
            jax.ShapeDtypeStruct((heads_all, own, LANES), F32),
            jax.ShapeDtypeStruct((own, LANES), F32),
            jax.ShapeDtypeStruct((width, heads_all * own), BF16),
        ],
        scratch_shapes=[
            pltpu.VMEM((n_seq, heads_all * own, keys), BF16),
            pltpu.VMEM((n_seq, own, keys), F32),
        ],
        compiler_params=limit(20),
        cost_estimate=product,
        name="key_grad",
    )(got, *all_keys)

    far = swap(far, "seq", n_seq, 1)
    near, term = pl.pallas_call(
        functools.partial(products_kernel, n_seq),
        in_specs=[vmem_spec()] * (2 + n_seq),
        out_specs=[vmem_spec()] * 2,
        out_shape=[
            jax.ShapeDtypeStruct((half, keys, width), F32),
            jax.ShapeDtypeStruct((heads_all * own, width), F32),
        ],
        compiler_params=limit(16),
        cost_estimate=product,
        name="products",
    )(gated, weighted, *all_keys)
    paired = [near[e] + far[e].astype(F32) for e in range(half)]
    sides = [x.astype(BF16) for x in paired[1:]]
    term, *sides = lax.optimization_barrier((term, *sides))
    mine = paired[0]
    for e in range(1, half):
        mine = mine + swap(sides[e - 1], "seq", n_seq, 2 * e).astype(F32)

    rows_out = pl.pallas_call(
        functools.partial(queries_kernel, n_head, own),
        in_specs=[vmem_spec()] * 4,
        out_specs=vmem_spec(),
        out_shape=jax.ShapeDtypeStruct((group, wide_cols), BF16),
        compiler_params=limit(16),
        cost_estimate=pl.CostEstimate(flops=0, bytes_accessed=2**21, transcendentals=0),
        name="query_grad",
    )(term, queries, wide, kl_rows)
    own_rows = lax.all_to_all(rows_out, "head", 0, 0, tiled=True)
    own_rows, _ = lax.optimization_barrier((own_rows, mine))
    steps = bits(n_head)
    for mask in steps[:-1]:
        mine = mine + swap(mine.astype(BF16), "head", n_head, mask).astype(F32)
    last = swap(mine.astype(BF16), "head", n_head, steps[-1])

    all_rows = {0: own_rows}
    for k in range(2, n_seq, 2):
        all_rows[k] = swap(all_rows[0], "seq", n_seq, k)
    for k in range(0, n_seq, 2):
        all_rows[k + 1] = swap(all_rows[k], "seq", n_seq, 1)
    grad_query_index, hw, kl = pl.pallas_call(
        functools.partial(place_kernel, n_seq),
        in_specs=[vmem_spec()] * n_seq,
        out_specs=[pl.BlockSpec(memory_space=pl.ANY)] * 3,
        out_shape=[
            jax.ShapeDtypeStruct((rows, heads * width), BF16),
            jax.ShapeDtypeStruct((heads, rows), BF16),
            jax.ShapeDtypeStruct((rows,), BF16),
        ],
        scratch_shapes=[
            pltpu.VMEM((rows, LANES), F32),
            pltpu.VMEM((heads, rows), BF16),
            pltpu.VMEM((rows,), BF16),
            pltpu.SemaphoreType.DMA((n_seq + 2,)),
        ],
        compiler_params=limit(4),
        cost_estimate=pl.CostEstimate(flops=0, bytes_accessed=8 * rows * wide_cols, transcendentals=0),
        name="place",
    )(*[all_rows[k] for k in range(n_seq)])
    grad_key_index = (mine + last.astype(F32)).astype(BF16)
    return kl, grad_query_index, hw.T, grad_key_index


def plain_local(query_mla, key_mla, lse, query_index, key_index, head_weight, query_pos, key_block):
    row_count = query_mla.shape[0]
    key_count = key_mla.shape[0]
    mla_heads = lse.shape[1]
    head_width = query_mla.shape[1] // mla_heads
    index_heads = head_weight.shape[1]
    index_width = key_index.shape[1]
    queries = query_mla.reshape(row_count, mla_heads, head_width)
    mla_keys = key_mla.reshape(key_count, mla_heads, head_width)
    positions = key_block[0] * key_count + jnp.arange(key_count, dtype=jnp.int32)
    valid = positions[None, :] <= query_pos[:, None]
    score = jnp.einsum(
        "thd,jhd->htj", queries, mla_keys, preferred_element_type=jnp.float32
    ) * head_width ** (-0.5)
    attention_part = jnp.sum(
        jnp.where(valid[None], jnp.exp(score - lse.T[:, :, None]), 0.0), axis=0
    )
    indexer_q = query_index.reshape(row_count, index_heads, index_width)
    dots = jnp.einsum("tid,jd->tij", indexer_q, key_index, preferred_element_type=jnp.float32)
    rectified = jnp.maximum(dots, 0.0)
    logit_part = jnp.sum(head_weight[:, :, None] * rectified, axis=1)
    attention, logit = lax.psum((attention_part, logit_part), "head")
    masked = jnp.where(valid, logit, -1e30)
    local_peak = jnp.max(masked, axis=1)
    peak = lax.pmax(local_peak, "seq")
    shifted = jnp.where(valid, jnp.exp(masked - peak[:, None]), 0.0)
    norm, total = lax.psum((jnp.sum(shifted, axis=1), jnp.sum(attention, axis=1)), "seq")
    target = attention / total[:, None]
    log_prob = masked - peak[:, None] - jnp.log(norm)[:, None]
    prob = jnp.where(valid, jnp.exp(log_prob), 0.0)
    log_target = jnp.log(jnp.where(valid, attention, 1.0)) - jnp.log(total)[:, None]
    kl_part = jnp.sum(jnp.where(valid, target * (log_target - log_prob), 0.0), axis=1)
    dlogit = jnp.where(valid, prob - target, 0.0).astype(jnp.bfloat16)
    grad_rows = dlogit.astype(jnp.float32)
    weight_part = jnp.sum(grad_rows[:, None, :] * rectified, axis=2)
    opened = dots > 0
    gated = jnp.where(opened, dlogit[:, None, :], 0)
    query_part = jnp.einsum(
        "tij,jd->tid", gated, key_index, preferred_element_type=jnp.float32
    ).reshape(row_count, index_heads * index_width)
    coef = jnp.where(opened, grad_rows[:, None, :] * head_weight[:, :, None], 0.0).astype(
        jnp.bfloat16
    )
    key_part = jnp.einsum("tij,tid->jd", coef, indexer_q, preferred_element_type=jnp.float32)
    grad_key_index = lax.psum(key_part, "head").astype(jnp.bfloat16)
    query_sum, weight_sum, kl_sum = lax.psum((query_part, weight_part, kl_part), "seq")
    scaled = query_sum.reshape(row_count, index_heads, index_width) * head_weight[:, :, None]
    grad_query_index = scaled.reshape(row_count, index_heads * index_width).astype(jnp.bfloat16)
    grad_head_weight = weight_sum.astype(jnp.bfloat16)
    kl = kl_sum.astype(jnp.bfloat16)
    return (kl, grad_query_index, grad_head_weight, grad_key_index)


def solution(mesh):
    placed = (
        P(None, "head"),
        P("seq", "head"),
        P(None, "head"),
        P(None, "head"),
        P("seq", None),
        P(None, "head"),
        P(),
        P("seq"),
    )
    n_seq, n_head = mesh.shape["seq"], mesh.shape["head"]

    def local(*args):
        rows, heads = args[0].shape[0], args[5].shape[1]
        paired = all(n & (n - 1) == 0 and n > 1 for n in (n_seq, n_head))
        if paired and rows == 8 * n_seq * n_head and heads % n_seq == 0:
            return fast_local(n_seq, n_head, *args)
        return plain_local(*args)

    return jax.shard_map(
        local,
        mesh=mesh,
        in_specs=placed,
        out_specs=(P(), P(None, "head"), P(None, "head"), P("seq", None)),
        check_vma=False,
    )
```

```python
import functools
import math

import jax
import jax.numpy as jnp
from jax import lax
from jax.experimental import pallas as pl
from jax.experimental.pallas import tpu as pltpu
from jax.sharding import PartitionSpec as P

BF16 = jnp.bfloat16
F32 = jnp.float32
LANES = 128
NT = (((1,), (1,)), ((), ()))


def vmem_spec():
    return pl.BlockSpec(memory_space=pltpu.VMEM)


def head_parts(heads, width):
    least = LANES // math.gcd(LANES, width)
    first = heads // 2 // least * least
    return [first, heads - first] if first > 0 else [heads]


def bits(n):
    return [1 << b for b in range(n.bit_length() - 1)]


def attention_kernel(
    parts, block_hbm, pos_hbm, q_hbm, k_hbm, lse_hbm, qi_hbm, hw_hbm, out_ref,
    block_ref, pos_ref, q_ref, k_ref, lse_ref, hw_ref, acc_ref, sems, part_sems
):
    rows, keys = q_ref.shape[0], k_ref.shape[0]
    mla_heads, heads = lse_ref.shape[0], hw_ref.shape[0]
    width = q_ref.shape[1] // mla_heads
    cols = out_ref.shape[1] - keys - LANES
    log2e = math.log2(math.e)
    scale = width ** (-0.5) * log2e
    small = [
        pltpu.make_async_copy(source, target, sems.at[i])
        for i, (source, target) in enumerate(((lse_hbm, lse_ref), (hw_hbm, hw_ref), (pos_hbm, pos_ref), (block_hbm, block_ref)))
    ]
    share_at = pl.ds(pl.multiple_of(lax.axis_index("seq") * cols, LANES), cols)
    share_copy = pltpu.make_async_copy(qi_hbm.at[:, share_at], out_ref.at[:, keys : keys + cols], sems.at[4])
    large = []
    first = 0
    for i, n in enumerate(parts):
        at = slice(first * width, (first + n) * width)
        large.append(
            (
                pltpu.make_async_copy(q_hbm.at[:, at], q_ref.at[:, at], part_sems.at[0, i]),
                pltpu.make_async_copy(k_hbm.at[:, at], k_ref.at[:, at], part_sems.at[1, i]),
            )
        )
        first += n
    for copy in large[0]:
        copy.start()
    for copy in small:
        copy.start()
    for pair in large[1:]:
        for copy in pair:
            copy.start()
    share_copy.start()
    for copy in small:
        copy.wait()
    first = 0
    for i, n in enumerate(parts):
        for copy in large[i]:
            copy.wait()
        total = None
        for a in range(first, first + n):
            low, high = a * width, (a + 1) * width
            start, stop = low // LANES * LANES, -(-high // LANES) * LANES
            q = q_ref[:, start:stop]
            if start != low or stop != high:
                at = lax.broadcasted_iota(jnp.int32, (1, stop - start), 1) + start
                q = jnp.where((at >= low) & (at < high), q, jnp.zeros_like(q))
            score = lax.dot_general(k_ref[:, start:stop], q, NT, preferred_element_type=F32)
            value = jnp.exp2(score * scale - lse_ref[a : a + 1, :] * log2e)
            total = value if total is None else total + value
        if first == 0:
            acc_ref[...] = total
        else:
            acc_ref[...] += total
        first += n
    position = block_ref[0] * keys + lax.broadcasted_iota(jnp.int32, (keys, rows), 0)
    valid = position <= pos_ref[...]
    largest = float(jnp.finfo(F32).max)
    least = jnp.min(jnp.where(valid, acc_ref[...], largest), axis=0, keepdims=True)
    least = jnp.where(least < largest, least, 0.0)
    share = jnp.where(valid, acc_ref[...] - least, -1.0)
    out_ref[:, :keys] = jnp.transpose(share).astype(BF16)
    padded = jnp.concatenate([hw_ref[...], jnp.zeros((LANES - heads, rows), F32)], axis=0)
    sub = lax.broadcasted_iota(jnp.int32, (LANES, rows), 0)
    terms = jnp.transpose(jnp.where(sub == heads, least, padded))
    high = terms.astype(BF16).astype(F32)
    rest = terms - high
    mid = rest.astype(BF16).astype(F32)
    side = high + pltpu.roll(mid, heads + 1, 1) + pltpu.roll(rest - mid, 2 * (heads + 1), 1)
    out_ref[:, keys + cols :] = side.astype(BF16)
    share_copy.wait()


def keys_kernel(n_seq, n_head, own, got_ref, *refs):
    key_refs = refs[:n_seq]
    far_ref, gated_ref, q_ref, wide_ref, kl_ref, weighted_ref, dots_ref, logit_ref = refs[n_seq:]
    s = lax.axis_index("seq")
    keys, width = key_refs[0].shape
    heads_all = wide_ref.shape[0]
    heads = heads_all // n_head
    per = heads // n_seq
    cols = per * width
    group = n_head * own

    def three(terms, i):
        return sum([terms[:, j : j + 1] for j in range(i + heads + 1, LANES, heads + 1)][:2], terms[:, i : i + 1])

    for ss in range(n_seq):
        for pair in range(0, n_head, 2):
            at = ss * group + pair * own
            both = got_ref[at : at + 2 * own, keys : keys + cols].astype(F32)
            for e in range(2):
                part = both[e * own : (e + 1) * own]
                tiles = [part[:, i * width : (i + 1) * width] for i in range(per)]
                first = ((pair + e) * heads + ss * per) * own
                q_ref[first : first + per * own, :] = jnp.concatenate(tiles, axis=0).astype(BF16)
    for pair in range(0, n_head, 2):
        both = got_ref[pair * own : (pair + 2) * own, keys + cols :].astype(F32)
        for e in range(2):
            side = both[e * own : (e + 1) * own]
            for i in range(heads):
                wide_ref[(pair + e) * heads + i] = jnp.broadcast_to(three(side, i), (own, LANES))
    for k in range(n_seq):
        dots = lax.dot_general(q_ref[...], key_refs[k][...], NT, preferred_element_type=F32)
        dots_ref[k] = dots.astype(BF16)
        cube = jnp.maximum(dots, 0.0).reshape(heads_all, own, keys)
        for c in range(0, keys, LANES):
            logit_ref[k, :, c : c + LANES] = jnp.sum(cube[:, :, c : c + LANES] * wide_ref[...], axis=0)
    shares, valids, logits = [], [], []
    peak = jnp.full((own, 1), -1e30, F32)
    for k in range(n_seq):
        src = pl.multiple_of((s ^ k) * group, group)
        cube = got_ref[pl.ds(src, group), :keys].astype(F32).reshape(n_head, own, keys)
        least = three(got_ref[pl.ds(src, group), keys + cols :].astype(F32), heads).reshape(n_head, own, 1)
        valid = cube[0] >= 0.0
        shares.append(jnp.where(valid, jnp.sum(cube, axis=0) + jnp.sum(least, axis=0), 0.0))
        valids.append(valid)
        logits.append(jnp.where(valid, logit_ref[k], -1e30))
        peak = jnp.maximum(peak, jnp.max(logits[k], axis=1, keepdims=True))

    def row_sum(parts):
        return jnp.sum(sum(parts[1:], parts[0]), axis=1, keepdims=True)

    total = row_sum(shares)
    norm = row_sum([jnp.where(v, jnp.exp(x - peak), 0.0) for v, x in zip(valids, logits)])
    log_norm, log_total = jnp.log(norm), jnp.log(total)
    weighted = jnp.transpose(q_ref[...].astype(F32) * wide_ref[...].reshape(q_ref.shape)).astype(BF16)
    weighted_ref[...] = weighted
    kls = []
    for k in range(n_seq):
        target = shares[k] / total
        log_prob = logits[k] - peak - log_norm
        prob = jnp.where(valids[k], jnp.exp(log_prob), 0.0)
        log_target = jnp.log(jnp.where(valids[k], shares[k], 1.0)) - log_total
        kls.append(jnp.where(valids[k], target * (log_target - log_prob), 0.0))
        dlogit = jnp.where(valids[k], prob - target, 0.0)
        twice = jnp.concatenate([dlogit, dlogit], axis=0).astype(BF16)
        cube = dots_ref[k].reshape(heads_all // 2, 2 * own, keys)
        gated = jnp.where(cube > 0, twice[None], jnp.zeros_like(twice)[None]).reshape(heads_all * own, keys)
        gated_ref[k] = gated
        if k % 2 == 1:
            side = jnp.dot(weighted, gated, preferred_element_type=F32)
            far_ref[k // 2] = jnp.transpose(side).astype(BF16)
    kl_ref[...] = jnp.broadcast_to(row_sum(kls), kl_ref.shape)


def products_kernel(n_seq, gated_ref, weighted_ref, *refs):
    key_refs, near_ref, term_ref = refs[:n_seq], refs[n_seq], refs[n_seq + 1]
    term = None
    for k in range(n_seq):
        if k % 2 == 0:
            side = jnp.dot(weighted_ref[...], gated_ref[k], preferred_element_type=F32)
            near_ref[k // 2] = jnp.transpose(side)
        part = jnp.dot(gated_ref[k], key_refs[k][...], preferred_element_type=F32)
        term = part if term is None else term + part
    term_ref[...] = term


def queries_kernel(n_head, own, term_ref, q_ref, wide_ref, kl_ref, out_ref):
    width = q_ref.shape[1]
    heads_all = wide_ref.shape[0]
    heads = heads_all // n_head
    term = term_ref[...]
    per_head = jnp.sum((term * q_ref[...].astype(F32)).reshape(heads_all, own, width), axis=2, keepdims=True)
    scaled = term.reshape(heads_all, own, width) * wide_ref[...]
    lane = lax.broadcasted_iota(jnp.int32, (own, LANES), 1)
    for pair in range(0, n_head, 2):
        rows = slice(pair * own, (pair + 2) * own)
        one, two = pair * heads, (pair + 1) * heads
        first = second = jnp.where(lane == heads, kl_ref[...], 0.0)
        for i in range(heads):
            both = jnp.concatenate([scaled[one + i], scaled[two + i]], axis=0)
            out_ref[rows, i * width : (i + 1) * width] = both.astype(BF16)
            first = jnp.where(lane == i, per_head[one + i], first)
            second = jnp.where(lane == i, per_head[two + i], second)
        out_ref[rows, heads * width :] = jnp.concatenate([first, second], axis=0).astype(BF16)


def place_kernel(n_seq, *refs):
    pieces = refs[:n_seq]
    gq_ref, hw_out, kl_out, side_ref, hw_ref, kl_ref, sems = refs[n_seq:]
    s = lax.axis_index("seq")
    rows, cols = pieces[0].shape[0], gq_ref.shape[1]
    heads = hw_ref.shape[0]
    copies = []
    for k in range(n_seq):
        at = pl.ds(pl.multiple_of((s ^ k) * rows, rows), rows)
        copies.append(pltpu.make_async_copy(pieces[k].at[:, :cols], gq_ref.at[at, :], sems.at[k]))
        copies[k].start()
        side_ref[at, :] = pieces[k][:, cols:].astype(F32)
    side = jnp.transpose(side_ref[...])
    hw_ref[...] = side[:heads, :].astype(BF16)
    kl_ref[...] = side[heads, :].astype(BF16)
    for source, target in ((hw_ref, hw_out), (kl_ref, kl_out)):
        copies.append(pltpu.make_async_copy(source, target, sems.at[len(copies)]))
        copies[-1].start()
    for copy in copies:
        copy.wait()


def fast_local(n_seq, n_head, query_mla, key_mla, lse, query_index, key_index, head_weight, query_pos, key_block):
    rows, keys = query_mla.shape[0], key_mla.shape[0]
    mla_heads = lse.shape[1]
    mla_width = query_mla.shape[1] // mla_heads
    heads, width = head_weight.shape[1], key_index.shape[1]
    own = rows // (n_seq * n_head)
    group = n_head * own
    heads_all = heads * n_head
    half = n_seq // 2
    wide_cols = heads * width + LANES

    def swap(x, axis, n, mask):
        return lax.ppermute(x, axis, [(i, i ^ mask) for i in range(n)])

    def limit(mib):
        return pltpu.CompilerParams(vmem_limit_bytes=mib * 2**20)

    cols = query_index.shape[1] // n_seq
    parts = head_parts(mla_heads, mla_width)
    hbm = pl.BlockSpec(memory_space=pltpu.HBM)
    sent = pl.pallas_call(
        functools.partial(attention_kernel, parts),
        in_specs=[hbm] * 7,
        out_specs=vmem_spec(),
        out_shape=jax.ShapeDtypeStruct((rows, keys + cols + LANES), BF16),
        scratch_shapes=[
            pltpu.SMEM((1,), jnp.int32),
            pltpu.VMEM((1, rows), jnp.int32),
            pltpu.VMEM(query_mla.shape, BF16),
            pltpu.VMEM(key_mla.shape, BF16),
            pltpu.VMEM((mla_heads, rows), F32),
            pltpu.VMEM((heads, rows), F32),
            pltpu.VMEM((keys, rows), F32),
            pltpu.SemaphoreType.DMA((5,)),
            pltpu.SemaphoreType.DMA((2, len(parts))),
        ],
        compiler_params=limit(56),
        cost_estimate=pl.CostEstimate(
            flops=4 * rows * keys * mla_heads * mla_width,
            bytes_accessed=2 * (rows + keys) * mla_heads * mla_width,
            transcendentals=rows * keys * mla_heads,
        ),
        name="attention",
    )(key_block, query_pos.reshape(1, rows), query_mla, key_mla, lse.T, query_index, head_weight.T)

    near_keys = [key_index] + [swap(key_index, "seq", n_seq, k) for k in range(2, n_seq, 2)]
    sent, *held = lax.optimization_barrier((sent, *near_keys[:-1]))
    near_keys = held + near_keys[-1:]
    got = lax.all_to_all(sent, ("seq", "head"), 0, 0, tiled=True)
    all_keys = []
    for piece in near_keys:
        all_keys += [piece, swap(piece, "seq", n_seq, 1)]

    product = pl.CostEstimate(
        flops=4 * own * heads_all * n_seq * keys * width, bytes_accessed=2**21, transcendentals=0
    )
    far, gated, queries, wide, kl_rows, weighted = pl.pallas_call(
        functools.partial(keys_kernel, n_seq, n_head, own),
        in_specs=[vmem_spec()] * (1 + n_seq),
        out_specs=[vmem_spec()] * 6,
        out_shape=[
            jax.ShapeDtypeStruct((half, keys, width), BF16),
            jax.ShapeDtypeStruct((n_seq, heads_all * own, keys), BF16),
            jax.ShapeDtypeStruct((heads_all * own, width), BF16),
            jax.ShapeDtypeStruct((heads_all, own, LANES), F32),
            jax.ShapeDtypeStruct((own, LANES), F32),
            jax.ShapeDtypeStruct((width, heads_all * own), BF16),
        ],
        scratch_shapes=[
            pltpu.VMEM((n_seq, heads_all * own, keys), BF16),
            pltpu.VMEM((n_seq, own, keys), F32),
        ],
        compiler_params=limit(20),
        cost_estimate=product,
        name="key_grad",
    )(got, *all_keys)

    far = swap(far, "seq", n_seq, 1)
    near, term = pl.pallas_call(
        functools.partial(products_kernel, n_seq),
        in_specs=[vmem_spec()] * (2 + n_seq),
        out_specs=[vmem_spec()] * 2,
        out_shape=[
            jax.ShapeDtypeStruct((half, keys, width), F32),
            jax.ShapeDtypeStruct((heads_all * own, width), F32),
        ],
        compiler_params=limit(16),
        cost_estimate=product,
        name="products",
    )(gated, weighted, *all_keys)
    paired = [near[e] + far[e].astype(F32) for e in range(half)]
    sides = [x.astype(BF16) for x in paired[1:]]
    term, *sides = lax.optimization_barrier((term, *sides))
    mine = paired[0]
    for e in range(1, half):
        mine = mine + swap(sides[e - 1], "seq", n_seq, 2 * e).astype(F32)

    rows_out = pl.pallas_call(
        functools.partial(queries_kernel, n_head, own),
        in_specs=[vmem_spec()] * 4,
        out_specs=vmem_spec(),
        out_shape=jax.ShapeDtypeStruct((group, wide_cols), BF16),
        compiler_params=limit(16),
        cost_estimate=pl.CostEstimate(flops=0, bytes_accessed=2**21, transcendentals=0),
        name="query_grad",
    )(term, queries, wide, kl_rows)
    own_rows = lax.all_to_all(rows_out, "head", 0, 0, tiled=True)
    own_rows, _ = lax.optimization_barrier((own_rows, mine))
    steps = bits(n_head)
    for mask in steps[:-1]:
        mine = mine + swap(mine.astype(BF16), "head", n_head, mask).astype(F32)
    last = swap(mine.astype(BF16), "head", n_head, steps[-1])

    all_rows = {0: own_rows}
    for k in range(2, n_seq, 2):
        all_rows[k] = swap(all_rows[0], "seq", n_seq, k)
    for k in range(0, n_seq, 2):
        all_rows[k + 1] = swap(all_rows[k], "seq", n_seq, 1)
    grad_query_index, hw, kl = pl.pallas_call(
        functools.partial(place_kernel, n_seq),
        in_specs=[vmem_spec()] * n_seq,
        out_specs=[pl.BlockSpec(memory_space=pl.ANY)] * 3,
        out_shape=[
            jax.ShapeDtypeStruct((rows, heads * width), BF16),
            jax.ShapeDtypeStruct((heads, rows), BF16),
            jax.ShapeDtypeStruct((rows,), BF16),
        ],
        scratch_shapes=[
            pltpu.VMEM((rows, LANES), F32),
            pltpu.VMEM((heads, rows), BF16),
            pltpu.VMEM((rows,), BF16),
            pltpu.SemaphoreType.DMA((n_seq + 2,)),
        ],
        compiler_params=limit(4),
        cost_estimate=pl.CostEstimate(flops=0, bytes_accessed=8 * rows * wide_cols, transcendentals=0),
        name="place",
    )(*[all_rows[k] for k in range(n_seq)])
    grad_key_index = (mine + last.astype(F32)).astype(BF16)
    return kl, grad_query_index, hw.T, grad_key_index


def plain_local(query_mla, key_mla, lse, query_index, key_index, head_weight, query_pos, key_block):
    row_count = query_mla.shape[0]
    key_count = key_mla.shape[0]
    mla_heads = lse.shape[1]
    head_width = query_mla.shape[1] // mla_heads
    index_heads = head_weight.shape[1]
    index_width = key_index.shape[1]
    queries = query_mla.reshape(row_count, mla_heads, head_width)
    mla_keys = key_mla.reshape(key_count, mla_heads, head_width)
    positions = key_block[0] * key_count + jnp.arange(key_count, dtype=jnp.int32)
    valid = positions[None, :] <= query_pos[:, None]
    score = jnp.einsum(
        "thd,jhd->htj", queries, mla_keys, preferred_element_type=jnp.float32
    ) * head_width ** (-0.5)
    attention_part = jnp.sum(
        jnp.where(valid[None], jnp.exp(score - lse.T[:, :, None]), 0.0), axis=0
    )
    indexer_q = query_index.reshape(row_count, index_heads, index_width)
    dots = jnp.einsum("tid,jd->tij", indexer_q, key_index, preferred_element_type=jnp.float32)
    rectified = jnp.maximum(dots, 0.0)
    logit_part = jnp.sum(head_weight[:, :, None] * rectified, axis=1)
    attention, logit = lax.psum((attention_part, logit_part), "head")
    masked = jnp.where(valid, logit, -1e30)
    local_peak = jnp.max(masked, axis=1)
    peak = lax.pmax(local_peak, "seq")
    shifted = jnp.where(valid, jnp.exp(masked - peak[:, None]), 0.0)
    norm, total = lax.psum((jnp.sum(shifted, axis=1), jnp.sum(attention, axis=1)), "seq")
    target = attention / total[:, None]
    log_prob = masked - peak[:, None] - jnp.log(norm)[:, None]
    prob = jnp.where(valid, jnp.exp(log_prob), 0.0)
    log_target = jnp.log(jnp.where(valid, attention, 1.0)) - jnp.log(total)[:, None]
    kl_part = jnp.sum(jnp.where(valid, target * (log_target - log_prob), 0.0), axis=1)
    dlogit = jnp.where(valid, prob - target, 0.0).astype(jnp.bfloat16)
    grad_rows = dlogit.astype(jnp.float32)
    weight_part = jnp.sum(grad_rows[:, None, :] * rectified, axis=2)
    opened = dots > 0
    gated = jnp.where(opened, dlogit[:, None, :], 0)
    query_part = jnp.einsum(
        "tij,jd->tid", gated, key_index, preferred_element_type=jnp.float32
    ).reshape(row_count, index_heads * index_width)
    coef = jnp.where(opened, grad_rows[:, None, :] * head_weight[:, :, None], 0.0).astype(
        jnp.bfloat16
    )
    key_part = jnp.einsum("tij,tid->jd", coef, indexer_q, preferred_element_type=jnp.float32)
    grad_key_index = lax.psum(key_part, "head").astype(jnp.bfloat16)
    query_sum, weight_sum, kl_sum = lax.psum((query_part, weight_part, kl_part), "seq")
    scaled = query_sum.reshape(row_count, index_heads, index_width) * head_weight[:, :, None]
    grad_query_index = scaled.reshape(row_count, index_heads * index_width).astype(jnp.bfloat16)
    grad_head_weight = weight_sum.astype(jnp.bfloat16)
    kl = kl_sum.astype(jnp.bfloat16)
    return (kl, grad_query_index, grad_head_weight, grad_key_index)


def solution(mesh):
    placed = (
        P(None, "head"),
        P("seq", "head"),
        P(None, "head"),
        P(None, "head"),
        P("seq", None),
        P(None, "head"),
        P(),
        P("seq"),
    )
    n_seq, n_head = mesh.shape["seq"], mesh.shape["head"]

    def local(*args):
        rows, heads = args[0].shape[0], args[5].shape[1]
        paired = all(n & (n - 1) == 0 and n > 1 for n in (n_seq, n_head))
        if paired and rows == 8 * n_seq * n_head and heads % n_seq == 0 and 3 * heads + 3 <= LANES:
            return fast_local(n_seq, n_head, *args)
        return plain_local(*args)

    return jax.shard_map(
        local,
        mesh=mesh,
        in_specs=placed,
        out_specs=(P(), P(None, "head"), P(None, "head"), P("seq", None)),
        check_vma=False,
    )
```

```python
import functools
import math

import jax
import jax.numpy as jnp
from jax import lax
from jax.experimental import pallas as pl
from jax.experimental.pallas import tpu as pltpu
from jax.sharding import PartitionSpec as P

BF16 = jnp.bfloat16
F32 = jnp.float32
LANES = 128
NT = (((1,), (1,)), ((), ()))


def vmem_spec():
    return pl.BlockSpec(memory_space=pltpu.VMEM)


def head_parts(heads, width):
    least = LANES // math.gcd(LANES, width)
    first = heads // 2 // least * least
    return [first, heads - first] if first > 0 else [heads]


def bits(n):
    return [1 << b for b in range(n.bit_length() - 1)]


def attention_kernel(
    parts, block_hbm, pos_hbm, q_hbm, k_hbm, lse_hbm, qi_hbm, hw_hbm, out_hbm,
    att_ref, side_ref, block_ref, pos_ref, q_ref, k_ref, lse_ref, hw_ref, acc_ref, sems, part_sems
):
    rows, keys = q_ref.shape[0], k_ref.shape[0]
    mla_heads, heads = lse_ref.shape[0], hw_ref.shape[0]
    width = q_ref.shape[1] // mla_heads
    cols = out_hbm.shape[1] - keys - LANES
    log2e = math.log2(math.e)
    scale = width ** (-0.5) * log2e
    small = [
        pltpu.make_async_copy(source, target, sems.at[i])
        for i, (source, target) in enumerate(((lse_hbm, lse_ref), (hw_hbm, hw_ref), (pos_hbm, pos_ref), (block_hbm, block_ref)))
    ]
    share_at = pl.ds(pl.multiple_of(lax.axis_index("seq") * cols, LANES), cols)
    share_copy = pltpu.make_async_copy(qi_hbm.at[:, share_at], out_hbm.at[:, keys : keys + cols], sems.at[4])
    large = []
    first = 0
    for i, n in enumerate(parts):
        at = slice(first * width, (first + n) * width)
        large.append(
            (
                pltpu.make_async_copy(q_hbm.at[:, at], q_ref.at[:, at], part_sems.at[0, i]),
                pltpu.make_async_copy(k_hbm.at[:, at], k_ref.at[:, at], part_sems.at[1, i]),
            )
        )
        first += n
    for copy in large[0]:
        copy.start()
    for copy in small:
        copy.start()
    for pair in large[1:]:
        for copy in pair:
            copy.start()
    share_copy.start()
    for copy in small:
        copy.wait()
    first = 0
    for i, n in enumerate(parts):
        for copy in large[i]:
            copy.wait()
        total = None
        for a in range(first, first + n):
            low, high = a * width, (a + 1) * width
            start, stop = low // LANES * LANES, -(-high // LANES) * LANES
            q = q_ref[:, start:stop]
            if start != low or stop != high:
                at = lax.broadcasted_iota(jnp.int32, (1, stop - start), 1) + start
                q = jnp.where((at >= low) & (at < high), q, jnp.zeros_like(q))
            score = lax.dot_general(k_ref[:, start:stop], q, NT, preferred_element_type=F32)
            value = jnp.exp2(score * scale - lse_ref[a : a + 1, :] * log2e)
            total = value if total is None else total + value
        if first == 0:
            acc_ref[...] = total
        else:
            acc_ref[...] += total
        first += n
    position = block_ref[0] * keys + lax.broadcasted_iota(jnp.int32, (keys, rows), 0)
    valid = position <= pos_ref[...]
    largest = float(jnp.finfo(F32).max)
    least = jnp.min(jnp.where(valid, acc_ref[...], largest), axis=0, keepdims=True)
    least = jnp.where(least < largest, least, 0.0)
    share = jnp.where(valid, acc_ref[...] - least, -1.0)
    copies = [share_copy]
    for i, at in enumerate((slice(0, rows // 2), slice(rows // 2, rows))):
        att_ref[at, :] = jnp.transpose(share[:, at]).astype(BF16)
        copies.append(pltpu.make_async_copy(att_ref.at[at, :], out_hbm.at[at, :keys], sems.at[5 + i]))
        copies[-1].start()
    padded = jnp.concatenate([hw_ref[...], jnp.zeros((LANES - heads, rows), F32)], axis=0)
    sub = lax.broadcasted_iota(jnp.int32, (LANES, rows), 0)
    terms = jnp.transpose(jnp.where(sub == heads, least, padded))
    high = terms.astype(BF16).astype(F32)
    rest = terms - high
    mid = rest.astype(BF16).astype(F32)
    side = high + pltpu.roll(mid, heads + 1, 1) + pltpu.roll(rest - mid, 2 * (heads + 1), 1)
    side_ref[...] = side.astype(BF16)
    copies.append(pltpu.make_async_copy(side_ref, out_hbm.at[:, keys + cols :], sems.at[7]))
    copies[-1].start()
    for copy in copies:
        copy.wait()


def keys_kernel(n_seq, n_head, own, got_ref, *refs):
    key_refs = refs[:n_seq]
    far_ref, gated_ref, q_ref, wide_ref, kl_ref, weighted_ref, dots_ref, logit_ref = refs[n_seq:]
    s = lax.axis_index("seq")
    keys, width = key_refs[0].shape
    heads_all = wide_ref.shape[0]
    heads = heads_all // n_head
    per = heads // n_seq
    cols = per * width
    group = n_head * own

    def three(terms, i):
        return sum([terms[:, j : j + 1] for j in range(i + heads + 1, LANES, heads + 1)][:2], terms[:, i : i + 1])

    for ss in range(n_seq):
        for pair in range(0, n_head, 2):
            at = ss * group + pair * own
            both = got_ref[at : at + 2 * own, keys : keys + cols].astype(F32)
            for e in range(2):
                part = both[e * own : (e + 1) * own]
                tiles = [part[:, i * width : (i + 1) * width] for i in range(per)]
                first = ((pair + e) * heads + ss * per) * own
                q_ref[first : first + per * own, :] = jnp.concatenate(tiles, axis=0).astype(BF16)
    for pair in range(0, n_head, 2):
        both = got_ref[pair * own : (pair + 2) * own, keys + cols :].astype(F32)
        for e in range(2):
            side = both[e * own : (e + 1) * own]
            for i in range(heads):
                wide_ref[(pair + e) * heads + i] = jnp.broadcast_to(three(side, i), (own, LANES))
    for k in range(n_seq):
        dots = lax.dot_general(q_ref[...], key_refs[k][...], NT, preferred_element_type=F32)
        dots_ref[k] = dots.astype(BF16)
        cube = jnp.maximum(dots, 0.0).reshape(heads_all, own, keys)
        for c in range(0, keys, LANES):
            logit_ref[k, :, c : c + LANES] = jnp.sum(cube[:, :, c : c + LANES] * wide_ref[...], axis=0)
    shares, valids, logits = [], [], []
    peak = jnp.full((own, 1), -1e30, F32)
    for k in range(n_seq):
        src = pl.multiple_of((s ^ k) * group, group)
        cube = got_ref[pl.ds(src, group), :keys].astype(F32).reshape(n_head, own, keys)
        least = three(got_ref[pl.ds(src, group), keys + cols :].astype(F32), heads).reshape(n_head, own, 1)
        valid = cube[0] >= 0.0
        shares.append(jnp.where(valid, jnp.sum(cube, axis=0) + jnp.sum(least, axis=0), 0.0))
        valids.append(valid)
        logits.append(jnp.where(valid, logit_ref[k], -1e30))
        peak = jnp.maximum(peak, jnp.max(logits[k], axis=1, keepdims=True))

    def row_sum(parts):
        return jnp.sum(sum(parts[1:], parts[0]), axis=1, keepdims=True)

    total = row_sum(shares)
    norm = row_sum([jnp.where(v, jnp.exp(x - peak), 0.0) for v, x in zip(valids, logits)])
    log_norm, log_total = jnp.log(norm), jnp.log(total)
    weighted = jnp.transpose(q_ref[...].astype(F32) * wide_ref[...].reshape(q_ref.shape)).astype(BF16)
    weighted_ref[...] = weighted
    kls = []
    for k in range(n_seq):
        target = shares[k] / total
        log_prob = logits[k] - peak - log_norm
        prob = jnp.where(valids[k], jnp.exp(log_prob), 0.0)
        log_target = jnp.log(jnp.where(valids[k], shares[k], 1.0)) - log_total
        kls.append(jnp.where(valids[k], target * (log_target - log_prob), 0.0))
        dlogit = jnp.where(valids[k], prob - target, 0.0)
        twice = jnp.concatenate([dlogit, dlogit], axis=0).astype(BF16)
        cube = dots_ref[k].reshape(heads_all // 2, 2 * own, keys)
        gated = jnp.where(cube > 0, twice[None], jnp.zeros_like(twice)[None]).reshape(heads_all * own, keys)
        gated_ref[k] = gated
        if k % 2 == 1:
            side = jnp.dot(weighted, gated, preferred_element_type=F32)
            far_ref[k // 2] = jnp.transpose(side).astype(BF16)
    kl_ref[...] = jnp.broadcast_to(row_sum(kls), kl_ref.shape)


def products_kernel(n_seq, n_head, gated_ref, weighted_ref, q_ref, kl_ref, *refs):
    key_refs, near_ref, term_ref, extra_ref = refs[:n_seq], refs[n_seq], refs[n_seq + 1], refs[n_seq + 2]
    own = kl_ref.shape[0]
    width = q_ref.shape[1]
    heads = q_ref.shape[0] // own // n_head
    term = None
    for k in range(n_seq):
        part = jnp.dot(gated_ref[k], key_refs[k][...], preferred_element_type=F32)
        term = part if term is None else term + part
    term_ref[...] = term
    for k in range(0, n_seq, 2):
        side = jnp.dot(weighted_ref[...], gated_ref[k], preferred_element_type=F32)
        near_ref[k // 2] = jnp.transpose(side)
    per_head = jnp.sum((term * q_ref[...].astype(F32)).reshape(n_head * heads, own, width), axis=2, keepdims=True)
    lane = lax.broadcasted_iota(jnp.int32, (own, LANES), 1)
    for h in range(n_head):
        extra = jnp.where(lane == heads, kl_ref[...], 0.0)
        for i in range(heads):
            extra = jnp.where(lane == i, per_head[h * heads + i], extra)
        extra_ref[h] = extra


def queries_kernel(n_head, own, term_ref, wide_ref, extra_ref, out_ref):
    width = term_ref.shape[1]
    heads_all = wide_ref.shape[0]
    heads = heads_all // n_head
    scaled = term_ref[...].reshape(heads_all, own, width) * wide_ref[...]
    for pair in range(0, n_head, 2):
        rows = slice(pair * own, (pair + 2) * own)
        one, two = pair * heads, (pair + 1) * heads
        for i in range(heads):
            both = jnp.concatenate([scaled[one + i], scaled[two + i]], axis=0)
            out_ref[rows, i * width : (i + 1) * width] = both.astype(BF16)
        out_ref[rows, heads * width :] = extra_ref[pair : pair + 2].reshape(2 * own, LANES).astype(BF16)


def place_kernel(n_seq, *refs):
    pieces = refs[:n_seq]
    gq_ref, hw_out, kl_out, side_ref, hw_ref, kl_ref, sems = refs[n_seq:]
    s = lax.axis_index("seq")
    rows, cols = pieces[0].shape[0], gq_ref.shape[1]
    heads = hw_ref.shape[0]
    copies = []
    for k in range(n_seq):
        at = pl.ds(pl.multiple_of((s ^ k) * rows, rows), rows)
        copies.append(pltpu.make_async_copy(pieces[k].at[:, :cols], gq_ref.at[at, :], sems.at[k]))
        copies[k].start()
        side_ref[at, :] = pieces[k][:, cols:].astype(F32)
    side = jnp.transpose(side_ref[...])
    hw_ref[...] = side[:heads, :].astype(BF16)
    kl_ref[...] = side[heads, :].astype(BF16)
    for source, target in ((hw_ref, hw_out), (kl_ref, kl_out)):
        copies.append(pltpu.make_async_copy(source, target, sems.at[len(copies)]))
        copies[-1].start()
    for copy in copies:
        copy.wait()


def fast_local(n_seq, n_head, query_mla, key_mla, lse, query_index, key_index, head_weight, query_pos, key_block):
    rows, keys = query_mla.shape[0], key_mla.shape[0]
    mla_heads = lse.shape[1]
    mla_width = query_mla.shape[1] // mla_heads
    heads, width = head_weight.shape[1], key_index.shape[1]
    own = rows // (n_seq * n_head)
    group = n_head * own
    heads_all = heads * n_head
    half = n_seq // 2
    wide_cols = heads * width + LANES

    def swap(x, axis, n, mask):
        return lax.ppermute(x, axis, [(i, i ^ mask) for i in range(n)])

    def limit(mib):
        return pltpu.CompilerParams(vmem_limit_bytes=mib * 2**20)

    cols = query_index.shape[1] // n_seq
    parts = head_parts(mla_heads, mla_width)
    hbm = pl.BlockSpec(memory_space=pltpu.HBM)
    sent = pl.pallas_call(
        functools.partial(attention_kernel, parts),
        in_specs=[hbm] * 7,
        out_specs=hbm,
        out_shape=jax.ShapeDtypeStruct((rows, keys + cols + LANES), BF16),
        scratch_shapes=[
            pltpu.VMEM((rows, keys), BF16),
            pltpu.VMEM((rows, LANES), BF16),
            pltpu.SMEM((1,), jnp.int32),
            pltpu.VMEM((1, rows), jnp.int32),
            pltpu.VMEM(query_mla.shape, BF16),
            pltpu.VMEM(key_mla.shape, BF16),
            pltpu.VMEM((mla_heads, rows), F32),
            pltpu.VMEM((heads, rows), F32),
            pltpu.VMEM((keys, rows), F32),
            pltpu.SemaphoreType.DMA((8,)),
            pltpu.SemaphoreType.DMA((2, len(parts))),
        ],
        compiler_params=limit(56),
        cost_estimate=pl.CostEstimate(
            flops=4 * rows * keys * mla_heads * mla_width,
            bytes_accessed=2 * (rows + keys) * mla_heads * mla_width,
            transcendentals=rows * keys * mla_heads,
        ),
        name="attention",
    )(key_block, query_pos.reshape(1, rows), query_mla, key_mla, lse.T, query_index, head_weight.T)

    near_keys = [key_index] + [swap(key_index, "seq", n_seq, k) for k in range(2, n_seq, 2)]
    sent, *held = lax.optimization_barrier((sent, *near_keys[:-1]))
    near_keys = held + near_keys[-1:]
    got = lax.all_to_all(sent, ("seq", "head"), 0, 0, tiled=True)
    all_keys = []
    for piece in near_keys:
        all_keys += [piece, swap(piece, "seq", n_seq, 1)]

    product = pl.CostEstimate(
        flops=4 * own * heads_all * n_seq * keys * width, bytes_accessed=2**21, transcendentals=0
    )
    far, gated, queries, wide, kl_rows, weighted = pl.pallas_call(
        functools.partial(keys_kernel, n_seq, n_head, own),
        in_specs=[vmem_spec()] * (1 + n_seq),
        out_specs=[vmem_spec()] * 6,
        out_shape=[
            jax.ShapeDtypeStruct((half, keys, width), BF16),
            jax.ShapeDtypeStruct((n_seq, heads_all * own, keys), BF16),
            jax.ShapeDtypeStruct((heads_all * own, width), BF16),
            jax.ShapeDtypeStruct((heads_all, own, LANES), F32),
            jax.ShapeDtypeStruct((own, LANES), F32),
            jax.ShapeDtypeStruct((width, heads_all * own), BF16),
        ],
        scratch_shapes=[
            pltpu.VMEM((n_seq, heads_all * own, keys), BF16),
            pltpu.VMEM((n_seq, own, keys), F32),
        ],
        compiler_params=limit(20),
        cost_estimate=product,
        name="key_grad",
    )(got, *all_keys)

    far = swap(far, "seq", n_seq, 1)
    near, term, extra = pl.pallas_call(
        functools.partial(products_kernel, n_seq, n_head),
        in_specs=[vmem_spec()] * (4 + n_seq),
        out_specs=[vmem_spec()] * 3,
        out_shape=[
            jax.ShapeDtypeStruct((half, keys, width), F32),
            jax.ShapeDtypeStruct((heads_all * own, width), F32),
            jax.ShapeDtypeStruct((n_head, own, LANES), F32),
        ],
        compiler_params=limit(16),
        cost_estimate=product,
        name="products",
    )(gated, weighted, queries, kl_rows, *all_keys)
    paired = [near[e] + far[e].astype(F32) for e in range(half)]
    sides = [x.astype(BF16) for x in paired[1:]]
    term, *sides = lax.optimization_barrier((term, *sides))
    mine = paired[0]
    for e in range(1, half):
        mine = mine + swap(sides[e - 1], "seq", n_seq, 2 * e).astype(F32)

    rows_out = pl.pallas_call(
        functools.partial(queries_kernel, n_head, own),
        in_specs=[vmem_spec()] * 3,
        out_specs=vmem_spec(),
        out_shape=jax.ShapeDtypeStruct((group, wide_cols), BF16),
        compiler_params=limit(16),
        cost_estimate=pl.CostEstimate(flops=0, bytes_accessed=2**21, transcendentals=0),
        name="query_grad",
    )(term, wide, extra)
    own_rows = lax.all_to_all(rows_out, "head", 0, 0, tiled=True)
    own_rows, _ = lax.optimization_barrier((own_rows, mine))
    steps = bits(n_head)
    for mask in steps[:-1]:
        mine = mine + swap(mine.astype(BF16), "head", n_head, mask).astype(F32)
    last = swap(mine.astype(BF16), "head", n_head, steps[-1])

    all_rows = {0: own_rows}
    for k in range(2, n_seq, 2):
        all_rows[k] = swap(all_rows[0], "seq", n_seq, k)
    for k in range(0, n_seq, 2):
        all_rows[k + 1] = swap(all_rows[k], "seq", n_seq, 1)
    grad_query_index, hw, kl = pl.pallas_call(
        functools.partial(place_kernel, n_seq),
        in_specs=[vmem_spec()] * n_seq,
        out_specs=[pl.BlockSpec(memory_space=pl.ANY)] * 3,
        out_shape=[
            jax.ShapeDtypeStruct((rows, heads * width), BF16),
            jax.ShapeDtypeStruct((heads, rows), BF16),
            jax.ShapeDtypeStruct((rows,), BF16),
        ],
        scratch_shapes=[
            pltpu.VMEM((rows, LANES), F32),
            pltpu.VMEM((heads, rows), BF16),
            pltpu.VMEM((rows,), BF16),
            pltpu.SemaphoreType.DMA((n_seq + 2,)),
        ],
        compiler_params=limit(4),
        cost_estimate=pl.CostEstimate(flops=0, bytes_accessed=8 * rows * wide_cols, transcendentals=0),
        name="place",
    )(*[all_rows[k] for k in range(n_seq)])
    grad_key_index = (mine + last.astype(F32)).astype(BF16)
    return kl, grad_query_index, hw.T, grad_key_index


def plain_local(query_mla, key_mla, lse, query_index, key_index, head_weight, query_pos, key_block):
    row_count = query_mla.shape[0]
    key_count = key_mla.shape[0]
    mla_heads = lse.shape[1]
    head_width = query_mla.shape[1] // mla_heads
    index_heads = head_weight.shape[1]
    index_width = key_index.shape[1]
    queries = query_mla.reshape(row_count, mla_heads, head_width)
    mla_keys = key_mla.reshape(key_count, mla_heads, head_width)
    positions = key_block[0] * key_count + jnp.arange(key_count, dtype=jnp.int32)
    valid = positions[None, :] <= query_pos[:, None]
    score = jnp.einsum(
        "thd,jhd->htj", queries, mla_keys, preferred_element_type=jnp.float32
    ) * head_width ** (-0.5)
    attention_part = jnp.sum(
        jnp.where(valid[None], jnp.exp(score - lse.T[:, :, None]), 0.0), axis=0
    )
    indexer_q = query_index.reshape(row_count, index_heads, index_width)
    dots = jnp.einsum("tid,jd->tij", indexer_q, key_index, preferred_element_type=jnp.float32)
    rectified = jnp.maximum(dots, 0.0)
    logit_part = jnp.sum(head_weight[:, :, None] * rectified, axis=1)
    attention, logit = lax.psum((attention_part, logit_part), "head")
    masked = jnp.where(valid, logit, -1e30)
    local_peak = jnp.max(masked, axis=1)
    peak = lax.pmax(local_peak, "seq")
    shifted = jnp.where(valid, jnp.exp(masked - peak[:, None]), 0.0)
    norm, total = lax.psum((jnp.sum(shifted, axis=1), jnp.sum(attention, axis=1)), "seq")
    target = attention / total[:, None]
    log_prob = masked - peak[:, None] - jnp.log(norm)[:, None]
    prob = jnp.where(valid, jnp.exp(log_prob), 0.0)
    log_target = jnp.log(jnp.where(valid, attention, 1.0)) - jnp.log(total)[:, None]
    kl_part = jnp.sum(jnp.where(valid, target * (log_target - log_prob), 0.0), axis=1)
    dlogit = jnp.where(valid, prob - target, 0.0).astype(jnp.bfloat16)
    grad_rows = dlogit.astype(jnp.float32)
    weight_part = jnp.sum(grad_rows[:, None, :] * rectified, axis=2)
    opened = dots > 0
    gated = jnp.where(opened, dlogit[:, None, :], 0)
    query_part = jnp.einsum(
        "tij,jd->tid", gated, key_index, preferred_element_type=jnp.float32
    ).reshape(row_count, index_heads * index_width)
    coef = jnp.where(opened, grad_rows[:, None, :] * head_weight[:, :, None], 0.0).astype(
        jnp.bfloat16
    )
    key_part = jnp.einsum("tij,tid->jd", coef, indexer_q, preferred_element_type=jnp.float32)
    grad_key_index = lax.psum(key_part, "head").astype(jnp.bfloat16)
    query_sum, weight_sum, kl_sum = lax.psum((query_part, weight_part, kl_part), "seq")
    scaled = query_sum.reshape(row_count, index_heads, index_width) * head_weight[:, :, None]
    grad_query_index = scaled.reshape(row_count, index_heads * index_width).astype(jnp.bfloat16)
    grad_head_weight = weight_sum.astype(jnp.bfloat16)
    kl = kl_sum.astype(jnp.bfloat16)
    return (kl, grad_query_index, grad_head_weight, grad_key_index)


def solution(mesh):
    placed = (
        P(None, "head"),
        P("seq", "head"),
        P(None, "head"),
        P(None, "head"),
        P("seq", None),
        P(None, "head"),
        P(),
        P("seq"),
    )
    n_seq, n_head = mesh.shape["seq"], mesh.shape["head"]

    def local(*args):
        rows, heads = args[0].shape[0], args[5].shape[1]
        paired = all(n & (n - 1) == 0 and n > 1 for n in (n_seq, n_head))
        if paired and rows == 8 * n_seq * n_head and heads % n_seq == 0 and 3 * heads + 3 <= LANES:
            return fast_local(n_seq, n_head, *args)
        return plain_local(*args)

    return jax.shard_map(
        local,
        mesh=mesh,
        in_specs=placed,
        out_specs=(P(), P(None, "head"), P(None, "head"), P("seq", None)),
        check_vma=False,
    )
```

```python
import functools
import math

import jax
import jax.numpy as jnp
from jax import lax
from jax.experimental import pallas as pl
from jax.experimental.pallas import tpu as pltpu
from jax.sharding import PartitionSpec as P

BF16 = jnp.bfloat16
F32 = jnp.float32
LANES = 128
NT = (((1,), (1,)), ((), ()))


def vmem_spec():
    return pl.BlockSpec(memory_space=pltpu.VMEM)


def head_parts(heads, width):
    least = LANES // math.gcd(LANES, width)
    first = heads // 2 // least * least
    return [first, heads - first] if first > 0 else [heads]


def bits(n):
    return [1 << b for b in range(n.bit_length() - 1)]


def attention_kernel(
    parts, block_hbm, pos_hbm, q_hbm, k_hbm, lse_hbm, qi_hbm, hw_hbm, out_hbm,
    att_ref, side_ref, block_ref, pos_ref, q_ref, k_ref, lse_ref, hw_ref, acc_ref, sems, part_sems
):
    rows, keys = q_ref.shape[0], k_ref.shape[0]
    mla_heads, heads = lse_ref.shape[0], hw_ref.shape[0]
    width = q_ref.shape[1] // mla_heads
    cols = out_hbm.shape[1] - keys - LANES
    log2e = math.log2(math.e)
    scale = width ** (-0.5) * log2e
    small = [
        pltpu.make_async_copy(source, target, sems.at[i])
        for i, (source, target) in enumerate(((lse_hbm, lse_ref), (hw_hbm, hw_ref), (pos_hbm, pos_ref), (block_hbm, block_ref)))
    ]
    share_at = pl.ds(pl.multiple_of(lax.axis_index("seq") * cols, LANES), cols)
    share_copy = pltpu.make_async_copy(qi_hbm.at[:, share_at], out_hbm.at[:, keys : keys + cols], sems.at[4])
    large = []
    first = 0
    for i, n in enumerate(parts):
        at = slice(first * width, (first + n) * width)
        large.append(
            (
                pltpu.make_async_copy(q_hbm.at[:, at], q_ref.at[:, at], part_sems.at[0, i]),
                pltpu.make_async_copy(k_hbm.at[:, at], k_ref.at[:, at], part_sems.at[1, i]),
            )
        )
        first += n
    for copy in large[0]:
        copy.start()
    for copy in small:
        copy.start()
    for pair in large[1:]:
        for copy in pair:
            copy.start()
    share_copy.start()
    for copy in small:
        copy.wait()
    first = 0
    for i, n in enumerate(parts):
        for copy in large[i]:
            copy.wait()
        total = None
        for a in range(first, first + n):
            low, high = a * width, (a + 1) * width
            start, stop = low // LANES * LANES, -(-high // LANES) * LANES
            q = q_ref[:, start:stop]
            if start != low or stop != high:
                at = lax.broadcasted_iota(jnp.int32, (1, stop - start), 1) + start
                q = jnp.where((at >= low) & (at < high), q, jnp.zeros_like(q))
            score = lax.dot_general(k_ref[:, start:stop], q, NT, preferred_element_type=F32)
            value = jnp.exp2(score * scale - lse_ref[a : a + 1, :] * log2e)
            total = value if total is None else total + value
        if first == 0:
            acc_ref[...] = total
        else:
            acc_ref[...] += total
        first += n
    position = block_ref[0] * keys + lax.broadcasted_iota(jnp.int32, (keys, rows), 0)
    valid = position <= pos_ref[...]
    largest = float(jnp.finfo(F32).max)
    least = jnp.min(jnp.where(valid, acc_ref[...], largest), axis=0, keepdims=True)
    least = jnp.where(least < largest, least, 0.0)
    share = jnp.where(valid, acc_ref[...] - least, -1.0)
    copies = [share_copy]
    for i, at in enumerate((slice(0, rows // 2), slice(rows // 2, rows))):
        att_ref[at, :] = jnp.transpose(share[:, at]).astype(BF16)
        copies.append(pltpu.make_async_copy(att_ref.at[at, :], out_hbm.at[at, :keys], sems.at[5 + i]))
        copies[-1].start()
    padded = jnp.concatenate([hw_ref[...], jnp.zeros((LANES - heads, rows), F32)], axis=0)
    sub = lax.broadcasted_iota(jnp.int32, (LANES, rows), 0)
    terms = jnp.transpose(jnp.where(sub == heads, least, padded))
    high = terms.astype(BF16).astype(F32)
    rest = terms - high
    mid = rest.astype(BF16).astype(F32)
    side = high + pltpu.roll(mid, heads + 1, 1) + pltpu.roll(rest - mid, 2 * (heads + 1), 1)
    side_ref[...] = side.astype(BF16)
    copies.append(pltpu.make_async_copy(side_ref, out_hbm.at[:, keys + cols :], sems.at[7]))
    copies[-1].start()
    for copy in copies:
        copy.wait()


def keys_kernel(n_seq, n_head, own, got_ref, *refs):
    key_refs = refs[:n_seq]
    far_ref, gated_ref, q_ref, wide_ref, kl_ref, weighted_ref, dots_ref, logit_ref = refs[n_seq:]
    s = lax.axis_index("seq")
    keys, width = key_refs[0].shape
    heads_all = wide_ref.shape[0]
    heads = heads_all // n_head
    per = heads // n_seq
    cols = per * width
    group = n_head * own

    def three(terms, i):
        return sum([terms[:, j : j + 1] for j in range(i + heads + 1, LANES, heads + 1)][:2], terms[:, i : i + 1])

    for ss in range(n_seq):
        for pair in range(0, n_head, 2):
            at = ss * group + pair * own
            both = got_ref[at : at + 2 * own, keys : keys + cols].astype(F32)
            for e in range(2):
                part = both[e * own : (e + 1) * own]
                tiles = [part[:, i * width : (i + 1) * width] for i in range(per)]
                first = ((pair + e) * heads + ss * per) * own
                q_ref[first : first + per * own, :] = jnp.concatenate(tiles, axis=0).astype(BF16)
    for pair in range(0, n_head, 2):
        both = got_ref[pair * own : (pair + 2) * own, keys + cols :].astype(F32)
        for e in range(2):
            side = both[e * own : (e + 1) * own]
            for i in range(heads):
                wide_ref[(pair + e) * heads + i] = jnp.broadcast_to(three(side, i), (own, LANES))
    for k in range(n_seq):
        dots = lax.dot_general(q_ref[...], key_refs[k][...], NT, preferred_element_type=F32)
        dots_ref[k] = dots.astype(BF16)
        cube = jnp.maximum(dots, 0.0).reshape(heads_all, own, keys)
        for c in range(0, keys, LANES):
            logit_ref[k, :, c : c + LANES] = jnp.sum(cube[:, :, c : c + LANES] * wide_ref[...], axis=0)
    shares, valids, logits = [], [], []
    peak = jnp.full((own, 1), -1e30, F32)
    for k in range(n_seq):
        src = pl.multiple_of((s ^ k) * group, group)
        cube = got_ref[pl.ds(src, group), :keys].astype(F32).reshape(n_head, own, keys)
        least = three(got_ref[pl.ds(src, group), keys + cols :].astype(F32), heads).reshape(n_head, own, 1)
        valid = cube[0] >= 0.0
        shares.append(jnp.where(valid, jnp.sum(cube, axis=0) + jnp.sum(least, axis=0), 0.0))
        valids.append(valid)
        logits.append(jnp.where(valid, logit_ref[k], -1e30))
        peak = jnp.maximum(peak, jnp.max(logits[k], axis=1, keepdims=True))

    def row_sum(parts):
        return jnp.sum(sum(parts[1:], parts[0]), axis=1, keepdims=True)

    total = row_sum(shares)
    norm = row_sum([jnp.where(v, jnp.exp(x - peak), 0.0) for v, x in zip(valids, logits)])
    log_norm, log_total = jnp.log(norm), jnp.log(total)
    weighted = jnp.transpose(q_ref[...].astype(F32) * wide_ref[...].reshape(q_ref.shape)).astype(BF16)
    weighted_ref[...] = weighted
    kls = []
    for k in range(n_seq):
        target = shares[k] / total
        log_prob = logits[k] - peak - log_norm
        prob = jnp.where(valids[k], jnp.exp(log_prob), 0.0)
        log_target = jnp.log(jnp.where(valids[k], shares[k], 1.0)) - log_total
        kls.append(jnp.where(valids[k], target * (log_target - log_prob), 0.0))
        dlogit = jnp.where(valids[k], prob - target, 0.0)
        twice = jnp.concatenate([dlogit, dlogit], axis=0).astype(BF16)
        cube = dots_ref[k].reshape(heads_all // 2, 2 * own, keys)
        gated = jnp.where(cube > 0, twice[None], jnp.zeros_like(twice)[None]).reshape(heads_all * own, keys)
        gated_ref[k] = gated
        if k % 2 == 1:
            side = jnp.dot(weighted, gated, preferred_element_type=F32)
            far_ref[k // 2] = jnp.transpose(side).astype(BF16)
    kl_ref[...] = jnp.broadcast_to(row_sum(kls), kl_ref.shape)


def products_kernel(n_seq, n_head, gated_ref, weighted_ref, q_ref, kl_ref, *refs):
    key_refs, near_ref, term_ref, extra_ref = refs[:n_seq], refs[n_seq], refs[n_seq + 1], refs[n_seq + 2]
    own = kl_ref.shape[0]
    width = q_ref.shape[1]
    heads = q_ref.shape[0] // own // n_head
    term = None
    for k in range(n_seq):
        part = jnp.dot(gated_ref[k], key_refs[k][...], preferred_element_type=F32)
        term = part if term is None else term + part
    term_ref[...] = term
    for k in range(0, n_seq, 2):
        side = jnp.dot(weighted_ref[...], gated_ref[k], preferred_element_type=F32)
        near_ref[k // 2] = jnp.transpose(side)
    per_head = jnp.sum((term * q_ref[...].astype(F32)).reshape(n_head * heads, own, width), axis=2, keepdims=True)
    lane = lax.broadcasted_iota(jnp.int32, (own, LANES), 1)
    for h in range(n_head):
        extra = jnp.where(lane == heads, kl_ref[...], 0.0)
        for i in range(heads):
            extra = jnp.where(lane == i, per_head[h * heads + i], extra)
        extra_ref[h] = extra


def queries_kernel(n_head, own, term_ref, wide_ref, extra_ref, out_ref):
    width = term_ref.shape[1]
    heads_all = wide_ref.shape[0]
    heads = heads_all // n_head
    scaled = term_ref[...].reshape(heads_all, own, width) * wide_ref[...]
    for pair in range(0, n_head, 2):
        rows = slice(pair * own, (pair + 2) * own)
        one, two = pair * heads, (pair + 1) * heads
        for i in range(heads):
            both = jnp.concatenate([scaled[one + i], scaled[two + i]], axis=0)
            out_ref[rows, i * width : (i + 1) * width] = both.astype(BF16)
        out_ref[rows, heads * width :] = extra_ref[pair : pair + 2].reshape(2 * own, LANES).astype(BF16)


def place_kernel(n_seq, *refs):
    pieces = refs[:n_seq]
    gq_ref, hw_out, kl_out, side_ref, hw_ref, kl_ref, sems = refs[n_seq:]
    s = lax.axis_index("seq")
    rows, cols = pieces[0].shape[0], gq_ref.shape[1]
    heads = hw_ref.shape[0]
    copies = []
    for k in range(n_seq):
        at = pl.ds(pl.multiple_of((s ^ k) * rows, rows), rows)
        copies.append(pltpu.make_async_copy(pieces[k].at[:, :cols], gq_ref.at[at, :], sems.at[k]))
        copies[k].start()
        side_ref[at, :] = pieces[k][:, cols:].astype(F32)
    side = jnp.transpose(side_ref[...])
    hw_ref[...] = side[:heads, :].astype(BF16)
    kl_ref[...] = side[heads, :].astype(BF16)
    for source, target in ((hw_ref, hw_out), (kl_ref, kl_out)):
        copies.append(pltpu.make_async_copy(source, target, sems.at[len(copies)]))
        copies[-1].start()
    for copy in copies:
        copy.wait()


def fast_local(n_seq, n_head, query_mla, key_mla, lse, query_index, key_index, head_weight, query_pos, key_block):
    rows, keys = query_mla.shape[0], key_mla.shape[0]
    mla_heads = lse.shape[1]
    mla_width = query_mla.shape[1] // mla_heads
    heads, width = head_weight.shape[1], key_index.shape[1]
    own = rows // (n_seq * n_head)
    group = n_head * own
    heads_all = heads * n_head
    half = n_seq // 2
    wide_cols = heads * width + LANES

    def swap(x, axis, n, mask):
        return lax.ppermute(x, axis, [(i, i ^ mask) for i in range(n)])

    def limit(mib):
        return pltpu.CompilerParams(vmem_limit_bytes=mib * 2**20)

    cols = query_index.shape[1] // n_seq
    parts = head_parts(mla_heads, mla_width)
    hbm = pl.BlockSpec(memory_space=pltpu.HBM)
    sent = pl.pallas_call(
        functools.partial(attention_kernel, parts),
        in_specs=[hbm] * 7,
        out_specs=hbm,
        out_shape=jax.ShapeDtypeStruct((rows, keys + cols + LANES), BF16),
        scratch_shapes=[
            pltpu.VMEM((rows, keys), BF16),
            pltpu.VMEM((rows, LANES), BF16),
            pltpu.SMEM((1,), jnp.int32),
            pltpu.VMEM((1, rows), jnp.int32),
            pltpu.VMEM(query_mla.shape, BF16),
            pltpu.VMEM(key_mla.shape, BF16),
            pltpu.VMEM((mla_heads, rows), F32),
            pltpu.VMEM((heads, rows), F32),
            pltpu.VMEM((keys, rows), F32),
            pltpu.SemaphoreType.DMA((8,)),
            pltpu.SemaphoreType.DMA((2, len(parts))),
        ],
        compiler_params=limit(56),
        cost_estimate=pl.CostEstimate(
            flops=4 * rows * keys * mla_heads * mla_width,
            bytes_accessed=2 * (rows + keys) * mla_heads * mla_width,
            transcendentals=rows * keys * mla_heads,
        ),
        name="attention",
    )(key_block, query_pos.reshape(1, rows), query_mla, key_mla, lse.T, query_index, head_weight.T)

    near_keys = [key_index] + [swap(key_index, "seq", n_seq, k) for k in range(2, n_seq, 2)]
    sent, *held = lax.optimization_barrier((sent, *near_keys[:-1]))
    near_keys = held + near_keys[-1:]
    got = lax.all_to_all(sent, ("seq", "head"), 0, 0, tiled=True)
    all_keys = []
    for piece in near_keys:
        all_keys += [piece, swap(piece, "seq", n_seq, 1)]

    product = pl.CostEstimate(
        flops=4 * own * heads_all * n_seq * keys * width, bytes_accessed=2**21, transcendentals=0
    )
    far, gated, queries, wide, kl_rows, weighted = pl.pallas_call(
        functools.partial(keys_kernel, n_seq, n_head, own),
        in_specs=[vmem_spec()] * (1 + n_seq),
        out_specs=[vmem_spec()] * 6,
        out_shape=[
            jax.ShapeDtypeStruct((half, keys, width), BF16),
            jax.ShapeDtypeStruct((n_seq, heads_all * own, keys), BF16),
            jax.ShapeDtypeStruct((heads_all * own, width), BF16),
            jax.ShapeDtypeStruct((heads_all, own, LANES), F32),
            jax.ShapeDtypeStruct((own, LANES), F32),
            jax.ShapeDtypeStruct((width, heads_all * own), BF16),
        ],
        scratch_shapes=[
            pltpu.VMEM((n_seq, heads_all * own, keys), BF16),
            pltpu.VMEM((n_seq, own, keys), F32),
        ],
        compiler_params=limit(20),
        cost_estimate=product,
        name="key_grad",
    )(got, *all_keys)

    far = swap(far, "seq", n_seq, 1)
    near, term, extra = pl.pallas_call(
        functools.partial(products_kernel, n_seq, n_head),
        in_specs=[vmem_spec()] * (4 + n_seq),
        out_specs=[vmem_spec()] * 3,
        out_shape=[
            jax.ShapeDtypeStruct((half, keys, width), F32),
            jax.ShapeDtypeStruct((heads_all * own, width), F32),
            jax.ShapeDtypeStruct((n_head, own, LANES), F32),
        ],
        compiler_params=limit(16),
        cost_estimate=product,
        name="products",
    )(gated, weighted, queries, kl_rows, *all_keys)
    paired = [near[e] + far[e].astype(F32) for e in range(half)]
    sides = [x.astype(BF16) for x in paired[1:]]
    term, *sides = lax.optimization_barrier((term, *sides))
    mine = paired[0]
    for e in reversed(range(1, half)):
        mine = mine + swap(sides[e - 1], "seq", n_seq, 2 * e).astype(F32)

    rows_out = pl.pallas_call(
        functools.partial(queries_kernel, n_head, own),
        in_specs=[vmem_spec()] * 3,
        out_specs=vmem_spec(),
        out_shape=jax.ShapeDtypeStruct((group, wide_cols), BF16),
        compiler_params=limit(16),
        cost_estimate=pl.CostEstimate(flops=0, bytes_accessed=2**21, transcendentals=0),
        name="query_grad",
    )(term, wide, extra)
    own_rows = lax.all_to_all(rows_out, "head", 0, 0, tiled=True)
    own_rows, _ = lax.optimization_barrier((own_rows, mine))
    steps = bits(n_head)
    for mask in steps[:-1]:
        mine = mine + swap(mine.astype(BF16), "head", n_head, mask).astype(F32)
    last = swap(mine.astype(BF16), "head", n_head, steps[-1])

    all_rows = {0: own_rows}
    for k in range(2, n_seq, 2):
        all_rows[k] = swap(all_rows[0], "seq", n_seq, k)
    for k in range(0, n_seq, 2):
        all_rows[k + 1] = swap(all_rows[k], "seq", n_seq, 1)
    grad_query_index, hw, kl = pl.pallas_call(
        functools.partial(place_kernel, n_seq),
        in_specs=[vmem_spec()] * n_seq,
        out_specs=[pl.BlockSpec(memory_space=pl.ANY)] * 3,
        out_shape=[
            jax.ShapeDtypeStruct((rows, heads * width), BF16),
            jax.ShapeDtypeStruct((heads, rows), BF16),
            jax.ShapeDtypeStruct((rows,), BF16),
        ],
        scratch_shapes=[
            pltpu.VMEM((rows, LANES), F32),
            pltpu.VMEM((heads, rows), BF16),
            pltpu.VMEM((rows,), BF16),
            pltpu.SemaphoreType.DMA((n_seq + 2,)),
        ],
        compiler_params=limit(4),
        cost_estimate=pl.CostEstimate(flops=0, bytes_accessed=8 * rows * wide_cols, transcendentals=0),
        name="place",
    )(*[all_rows[k] for k in range(n_seq)])
    grad_key_index = (mine + last.astype(F32)).astype(BF16)
    return kl, grad_query_index, hw.T, grad_key_index


def plain_local(query_mla, key_mla, lse, query_index, key_index, head_weight, query_pos, key_block):
    row_count = query_mla.shape[0]
    key_count = key_mla.shape[0]
    mla_heads = lse.shape[1]
    head_width = query_mla.shape[1] // mla_heads
    index_heads = head_weight.shape[1]
    index_width = key_index.shape[1]
    queries = query_mla.reshape(row_count, mla_heads, head_width)
    mla_keys = key_mla.reshape(key_count, mla_heads, head_width)
    positions = key_block[0] * key_count + jnp.arange(key_count, dtype=jnp.int32)
    valid = positions[None, :] <= query_pos[:, None]
    score = jnp.einsum(
        "thd,jhd->htj", queries, mla_keys, preferred_element_type=jnp.float32
    ) * head_width ** (-0.5)
    attention_part = jnp.sum(
        jnp.where(valid[None], jnp.exp(score - lse.T[:, :, None]), 0.0), axis=0
    )
    indexer_q = query_index.reshape(row_count, index_heads, index_width)
    dots = jnp.einsum("tid,jd->tij", indexer_q, key_index, preferred_element_type=jnp.float32)
    rectified = jnp.maximum(dots, 0.0)
    logit_part = jnp.sum(head_weight[:, :, None] * rectified, axis=1)
    attention, logit = lax.psum((attention_part, logit_part), "head")
    masked = jnp.where(valid, logit, -1e30)
    local_peak = jnp.max(masked, axis=1)
    peak = lax.pmax(local_peak, "seq")
    shifted = jnp.where(valid, jnp.exp(masked - peak[:, None]), 0.0)
    norm, total = lax.psum((jnp.sum(shifted, axis=1), jnp.sum(attention, axis=1)), "seq")
    target = attention / total[:, None]
    log_prob = masked - peak[:, None] - jnp.log(norm)[:, None]
    prob = jnp.where(valid, jnp.exp(log_prob), 0.0)
    log_target = jnp.log(jnp.where(valid, attention, 1.0)) - jnp.log(total)[:, None]
    kl_part = jnp.sum(jnp.where(valid, target * (log_target - log_prob), 0.0), axis=1)
    dlogit = jnp.where(valid, prob - target, 0.0).astype(jnp.bfloat16)
    grad_rows = dlogit.astype(jnp.float32)
    weight_part = jnp.sum(grad_rows[:, None, :] * rectified, axis=2)
    opened = dots > 0
    gated = jnp.where(opened, dlogit[:, None, :], 0)
    query_part = jnp.einsum(
        "tij,jd->tid", gated, key_index, preferred_element_type=jnp.float32
    ).reshape(row_count, index_heads * index_width)
    coef = jnp.where(opened, grad_rows[:, None, :] * head_weight[:, :, None], 0.0).astype(
        jnp.bfloat16
    )
    key_part = jnp.einsum("tij,tid->jd", coef, indexer_q, preferred_element_type=jnp.float32)
    grad_key_index = lax.psum(key_part, "head").astype(jnp.bfloat16)
    query_sum, weight_sum, kl_sum = lax.psum((query_part, weight_part, kl_part), "seq")
    scaled = query_sum.reshape(row_count, index_heads, index_width) * head_weight[:, :, None]
    grad_query_index = scaled.reshape(row_count, index_heads * index_width).astype(jnp.bfloat16)
    grad_head_weight = weight_sum.astype(jnp.bfloat16)
    kl = kl_sum.astype(jnp.bfloat16)
    return (kl, grad_query_index, grad_head_weight, grad_key_index)


def solution(mesh):
    placed = (
        P(None, "head"),
        P("seq", "head"),
        P(None, "head"),
        P(None, "head"),
        P("seq", None),
        P(None, "head"),
        P(),
        P("seq"),
    )
    n_seq, n_head = mesh.shape["seq"], mesh.shape["head"]

    def local(*args):
        rows, heads = args[0].shape[0], args[5].shape[1]
        paired = all(n & (n - 1) == 0 and n > 1 for n in (n_seq, n_head))
        if paired and rows == 8 * n_seq * n_head and heads % n_seq == 0 and 3 * heads + 3 <= LANES:
            return fast_local(n_seq, n_head, *args)
        return plain_local(*args)

    return jax.shard_map(
        local,
        mesh=mesh,
        in_specs=placed,
        out_specs=(P(), P(None, "head"), P(None, "head"), P("seq", None)),
        check_vma=False,
    )
```

```python
import functools
import math

import jax
import jax.numpy as jnp
from jax import lax
from jax.experimental import pallas as pl
from jax.experimental.pallas import tpu as pltpu
from jax.sharding import PartitionSpec as P

BF16 = jnp.bfloat16
F32 = jnp.float32
LANES = 128
NT = (((1,), (1,)), ((), ()))


def vmem_spec():
    return pl.BlockSpec(memory_space=pltpu.VMEM)


def head_parts(heads, width):
    least = LANES // math.gcd(LANES, width)
    first = heads // 2 // least * least
    return [first, heads - first] if first > 0 else [heads]


def bits(n):
    return [1 << b for b in range(n.bit_length() - 1)]


def attention_kernel(
    parts, block_hbm, pos_hbm, q_hbm, k_hbm, lse_hbm, qi_hbm, hw_hbm, out_hbm,
    att_ref, side_ref, block_ref, pos_ref, q_ref, k_ref, lse_ref, hw_ref, acc_ref, sems, part_sems
):
    rows, keys = q_ref.shape[0], k_ref.shape[0]
    mla_heads, heads = lse_ref.shape[0], hw_ref.shape[0]
    width = q_ref.shape[1] // mla_heads
    cols = out_hbm.shape[1] - keys - LANES
    log2e = math.log2(math.e)
    scale = width ** (-0.5) * log2e
    small = [
        pltpu.make_async_copy(source, target, sems.at[i])
        for i, (source, target) in enumerate(((lse_hbm, lse_ref), (hw_hbm, hw_ref), (pos_hbm, pos_ref), (block_hbm, block_ref)))
    ]
    share_at = pl.ds(pl.multiple_of(lax.axis_index("seq") * cols, LANES), cols)
    share_copy = pltpu.make_async_copy(qi_hbm.at[:, share_at], out_hbm.at[:, keys : keys + cols], sems.at[4])
    large = []
    first = 0
    for i, n in enumerate(parts):
        at = slice(first * width, (first + n) * width)
        large.append(
            (
                pltpu.make_async_copy(q_hbm.at[:, at], q_ref.at[:, at], part_sems.at[0, i]),
                pltpu.make_async_copy(k_hbm.at[:, at], k_ref.at[:, at], part_sems.at[1, i]),
            )
        )
        first += n
    for copy in large[0]:
        copy.start()
    for copy in small:
        copy.start()
    for pair in large[1:]:
        for copy in pair:
            copy.start()
    share_copy.start()
    for copy in small:
        copy.wait()
    first = 0
    for i, n in enumerate(parts):
        for copy in large[i]:
            copy.wait()
        total = None
        for a in range(first, first + n):
            low, high = a * width, (a + 1) * width
            start, stop = low // LANES * LANES, -(-high // LANES) * LANES
            q = q_ref[:, start:stop]
            if start != low or stop != high:
                at = lax.broadcasted_iota(jnp.int32, (1, stop - start), 1) + start
                q = jnp.where((at >= low) & (at < high), q, jnp.zeros_like(q))
            score = lax.dot_general(k_ref[:, start:stop], q, NT, preferred_element_type=F32)
            value = jnp.exp2(score * scale - lse_ref[a : a + 1, :] * log2e)
            total = value if total is None else total + value
        if first == 0:
            acc_ref[...] = total
        else:
            acc_ref[...] += total
        first += n
    position = block_ref[0] * keys + lax.broadcasted_iota(jnp.int32, (keys, rows), 0)
    valid = position <= pos_ref[...]
    largest = float(jnp.finfo(F32).max)
    least = jnp.min(jnp.where(valid, acc_ref[...], largest), axis=0, keepdims=True)
    least = jnp.where(least < largest, least, 0.0)
    share = jnp.where(valid, acc_ref[...] - least, -1.0)
    copies = [share_copy]
    for i, at in enumerate((slice(0, rows // 2), slice(rows // 2, rows))):
        att_ref[at, :] = jnp.transpose(share[:, at]).astype(BF16)
        copies.append(pltpu.make_async_copy(att_ref.at[at, :], out_hbm.at[at, :keys], sems.at[5 + i]))
        copies[-1].start()
    padded = jnp.concatenate([hw_ref[...], jnp.zeros((LANES - heads, rows), F32)], axis=0)
    sub = lax.broadcasted_iota(jnp.int32, (LANES, rows), 0)
    terms = jnp.transpose(jnp.where(sub == heads, least, padded))
    high = terms.astype(BF16).astype(F32)
    rest = terms - high
    mid = rest.astype(BF16).astype(F32)
    side = high + pltpu.roll(mid, heads + 1, 1) + pltpu.roll(rest - mid, 2 * (heads + 1), 1)
    side_ref[...] = side.astype(BF16)
    copies.append(pltpu.make_async_copy(side_ref, out_hbm.at[:, keys + cols :], sems.at[7]))
    copies[-1].start()
    for copy in copies:
        copy.wait()


def keys_kernel(n_seq, n_head, own, got_ref, *refs):
    key_refs = refs[:n_seq]
    far_ref, gated_ref, q_ref, wide_ref, kl_ref, weighted_ref, dots_ref, logit_ref = refs[n_seq:]
    s = lax.axis_index("seq")
    keys, width = key_refs[0].shape
    heads_all = wide_ref.shape[0]
    heads = heads_all // n_head
    per = heads // n_seq
    cols = per * width
    group = n_head * own

    def three(terms, i):
        return sum([terms[:, j : j + 1] for j in range(i + heads + 1, LANES, heads + 1)][:2], terms[:, i : i + 1])

    for ss in range(n_seq):
        for pair in range(0, n_head, 2):
            at = ss * group + pair * own
            both = got_ref[at : at + 2 * own, keys : keys + cols].astype(F32)
            for e in range(2):
                part = both[e * own : (e + 1) * own]
                tiles = [part[:, i * width : (i + 1) * width] for i in range(per)]
                first = ((pair + e) * heads + ss * per) * own
                q_ref[first : first + per * own, :] = jnp.concatenate(tiles, axis=0).astype(BF16)
    for pair in range(0, n_head, 2):
        both = got_ref[pair * own : (pair + 2) * own, keys + cols :].astype(F32)
        for e in range(2):
            side = both[e * own : (e + 1) * own]
            for i in range(heads):
                wide_ref[(pair + e) * heads + i] = jnp.broadcast_to(three(side, i), (own, LANES))
    for k in range(n_seq):
        dots = lax.dot_general(q_ref[...], key_refs[k][...], NT, preferred_element_type=F32)
        dots_ref[k] = dots.astype(BF16)
        cube = jnp.maximum(dots, 0.0).reshape(heads_all, own, keys)
        for c in range(0, keys, LANES):
            logit_ref[k, :, c : c + LANES] = jnp.sum(cube[:, :, c : c + LANES] * wide_ref[...], axis=0)
    shares, valids, logits = [], [], []
    peak = jnp.full((own, 1), -1e30, F32)
    for k in range(n_seq):
        src = pl.multiple_of((s ^ k) * group, group)
        cube = got_ref[pl.ds(src, group), :keys].astype(F32).reshape(n_head, own, keys)
        least = three(got_ref[pl.ds(src, group), keys + cols :].astype(F32), heads).reshape(n_head, own, 1)
        valid = cube[0] >= 0.0
        shares.append(jnp.where(valid, jnp.sum(cube, axis=0) + jnp.sum(least, axis=0), 0.0))
        valids.append(valid)
        logits.append(jnp.where(valid, logit_ref[k], -1e30))
        peak = jnp.maximum(peak, jnp.max(logits[k], axis=1, keepdims=True))

    def row_sum(parts):
        return jnp.sum(sum(parts[1:], parts[0]), axis=1, keepdims=True)

    total = row_sum(shares)
    norm = row_sum([jnp.where(v, jnp.exp(x - peak), 0.0) for v, x in zip(valids, logits)])
    log_norm, log_total = jnp.log(norm), jnp.log(total)
    weighted = jnp.transpose(q_ref[...].astype(F32) * wide_ref[...].reshape(q_ref.shape)).astype(BF16)
    weighted_ref[...] = weighted
    kls = []
    for k in range(n_seq):
        target = shares[k] / total
        log_prob = logits[k] - peak - log_norm
        prob = jnp.where(valids[k], jnp.exp(log_prob), 0.0)
        log_target = jnp.log(jnp.where(valids[k], shares[k], 1.0)) - log_total
        kls.append(jnp.where(valids[k], target * (log_target - log_prob), 0.0))
        dlogit = jnp.where(valids[k], prob - target, 0.0)
        twice = jnp.concatenate([dlogit, dlogit], axis=0).astype(BF16)
        cube = dots_ref[k].reshape(heads_all // 2, 2 * own, keys)
        gated = jnp.where(cube > 0, twice[None], jnp.zeros_like(twice)[None]).reshape(heads_all * own, keys)
        gated_ref[k] = gated
        if k % 2 == 1:
            side = jnp.dot(weighted, gated, preferred_element_type=F32)
            far_ref[k // 2] = jnp.transpose(side).astype(BF16)
    kl_ref[...] = jnp.broadcast_to(row_sum(kls), kl_ref.shape)


def products_kernel(n_seq, n_head, gated_ref, weighted_ref, q_ref, kl_ref, *refs):
    key_refs, near_ref, term_ref, extra_ref = refs[:n_seq], refs[n_seq], refs[n_seq + 1], refs[n_seq + 2]
    own = kl_ref.shape[0]
    width = q_ref.shape[1]
    heads = q_ref.shape[0] // own // n_head
    term = None
    for k in range(n_seq):
        part = jnp.dot(gated_ref[k], key_refs[k][...], preferred_element_type=F32)
        term = part if term is None else term + part
    term_ref[...] = term
    for k in range(0, n_seq, 2):
        side = jnp.dot(weighted_ref[...], gated_ref[k], preferred_element_type=F32)
        near_ref[k // 2] = jnp.transpose(side)
    per_head = jnp.sum((term * q_ref[...].astype(F32)).reshape(n_head * heads, own, width), axis=2, keepdims=True)
    lane = lax.broadcasted_iota(jnp.int32, (own, LANES), 1)
    for h in range(n_head):
        extra = jnp.where(lane == heads, kl_ref[...], 0.0)
        for i in range(heads):
            extra = jnp.where(lane == i, per_head[h * heads + i], extra)
        extra_ref[h] = extra


def queries_kernel(n_head, own, term_ref, wide_ref, extra_ref, out_ref):
    width = term_ref.shape[1]
    heads_all = wide_ref.shape[0]
    heads = heads_all // n_head
    scaled = term_ref[...].reshape(heads_all, own, width) * wide_ref[...]
    for pair in range(0, n_head, 2):
        rows = slice(pair * own, (pair + 2) * own)
        one, two = pair * heads, (pair + 1) * heads
        for i in range(heads):
            both = jnp.concatenate([scaled[one + i], scaled[two + i]], axis=0)
            out_ref[rows, i * width : (i + 1) * width] = both.astype(BF16)
        out_ref[rows, heads * width :] = extra_ref[pair : pair + 2].reshape(2 * own, LANES).astype(BF16)


def place_kernel(n_seq, *refs):
    pieces = refs[:n_seq]
    gq_ref, hw_out, kl_out, side_ref, hw_ref, kl_ref, sems = refs[n_seq:]
    s = lax.axis_index("seq")
    rows, cols = pieces[0].shape[0], gq_ref.shape[1]
    heads = hw_ref.shape[0]
    copies = []
    for k in range(n_seq):
        at = pl.ds(pl.multiple_of((s ^ k) * rows, rows), rows)
        copies.append(pltpu.make_async_copy(pieces[k].at[:, :cols], gq_ref.at[at, :], sems.at[k]))
        copies[k].start()
        side_ref[at, :] = pieces[k][:, cols:].astype(F32)
    side = jnp.transpose(side_ref[...])
    hw_ref[...] = side[:heads, :].astype(BF16)
    kl_ref[...] = side[heads, :].astype(BF16)
    for source, target in ((hw_ref, hw_out), (kl_ref, kl_out)):
        copies.append(pltpu.make_async_copy(source, target, sems.at[len(copies)]))
        copies[-1].start()
    for copy in copies:
        copy.wait()


def fast_local(n_seq, n_head, query_mla, key_mla, lse, query_index, key_index, head_weight, query_pos, key_block):
    rows, keys = query_mla.shape[0], key_mla.shape[0]
    mla_heads = lse.shape[1]
    mla_width = query_mla.shape[1] // mla_heads
    heads, width = head_weight.shape[1], key_index.shape[1]
    own = rows // (n_seq * n_head)
    group = n_head * own
    heads_all = heads * n_head
    half = n_seq // 2
    wide_cols = heads * width + LANES

    def swap(x, axis, n, mask):
        return lax.ppermute(x, axis, [(i, i ^ mask) for i in range(n)])

    def limit(mib):
        return pltpu.CompilerParams(vmem_limit_bytes=mib * 2**20)

    cols = query_index.shape[1] // n_seq
    parts = head_parts(mla_heads, mla_width)
    hbm = pl.BlockSpec(memory_space=pltpu.HBM)
    sent = pl.pallas_call(
        functools.partial(attention_kernel, parts),
        in_specs=[hbm] * 7,
        out_specs=hbm,
        out_shape=jax.ShapeDtypeStruct((rows, keys + cols + LANES), BF16),
        scratch_shapes=[
            pltpu.VMEM((rows, keys), BF16),
            pltpu.VMEM((rows, LANES), BF16),
            pltpu.SMEM((1,), jnp.int32),
            pltpu.VMEM((1, rows), jnp.int32),
            pltpu.VMEM(query_mla.shape, BF16),
            pltpu.VMEM(key_mla.shape, BF16),
            pltpu.VMEM((mla_heads, rows), F32),
            pltpu.VMEM((heads, rows), F32),
            pltpu.VMEM((keys, rows), F32),
            pltpu.SemaphoreType.DMA((8,)),
            pltpu.SemaphoreType.DMA((2, len(parts))),
        ],
        compiler_params=limit(56),
        cost_estimate=pl.CostEstimate(
            flops=4 * rows * keys * mla_heads * mla_width,
            bytes_accessed=2 * (rows + keys) * mla_heads * mla_width,
            transcendentals=rows * keys * mla_heads,
        ),
        name="attention",
    )(key_block, query_pos.reshape(1, rows), query_mla, key_mla, lse.T, query_index, head_weight.T)

    near_keys = [key_index] + [swap(key_index, "seq", n_seq, k) for k in range(2, n_seq, 2)]
    sent, *held = lax.optimization_barrier((sent, *near_keys[:-1]))
    near_keys = held + near_keys[-1:]
    got = lax.all_to_all(sent, ("seq", "head"), 0, 0, tiled=True)
    all_keys = []
    for piece in near_keys:
        all_keys += [piece, swap(piece, "seq", n_seq, 1)]

    product = pl.CostEstimate(
        flops=4 * own * heads_all * n_seq * keys * width, bytes_accessed=2**21, transcendentals=0
    )
    far, gated, queries, wide, kl_rows, weighted = pl.pallas_call(
        functools.partial(keys_kernel, n_seq, n_head, own),
        in_specs=[vmem_spec()] * (1 + n_seq),
        out_specs=[vmem_spec()] * 6,
        out_shape=[
            jax.ShapeDtypeStruct((half, keys, width), BF16),
            jax.ShapeDtypeStruct((n_seq, heads_all * own, keys), BF16),
            jax.ShapeDtypeStruct((heads_all * own, width), BF16),
            jax.ShapeDtypeStruct((heads_all, own, LANES), F32),
            jax.ShapeDtypeStruct((own, LANES), F32),
            jax.ShapeDtypeStruct((width, heads_all * own), BF16),
        ],
        scratch_shapes=[
            pltpu.VMEM((n_seq, heads_all * own, keys), BF16),
            pltpu.VMEM((n_seq, own, keys), F32),
        ],
        compiler_params=limit(20),
        cost_estimate=product,
        name="key_grad",
    )(got, *all_keys)

    far = swap(far, "seq", n_seq, 1)
    near, term, extra = pl.pallas_call(
        functools.partial(products_kernel, n_seq, n_head),
        in_specs=[vmem_spec()] * (4 + n_seq),
        out_specs=[vmem_spec()] * 3,
        out_shape=[
            jax.ShapeDtypeStruct((half, keys, width), F32),
            jax.ShapeDtypeStruct((heads_all * own, width), F32),
            jax.ShapeDtypeStruct((n_head, own, LANES), F32),
        ],
        compiler_params=limit(16),
        cost_estimate=product,
        name="products",
    )(gated, weighted, queries, kl_rows, *all_keys)
    paired = [near[e] + far[e].astype(F32) for e in range(half)]
    sides = [x.astype(BF16) for x in paired[1:]]
    term, *sides = lax.optimization_barrier((term, *sides))
    mine = paired[0]
    for e in [half - 1, *range(1, half - 1)]:
        mine = mine + swap(sides[e - 1], "seq", n_seq, 2 * e).astype(F32)

    rows_out = pl.pallas_call(
        functools.partial(queries_kernel, n_head, own),
        in_specs=[vmem_spec()] * 3,
        out_specs=vmem_spec(),
        out_shape=jax.ShapeDtypeStruct((group, wide_cols), BF16),
        compiler_params=limit(16),
        cost_estimate=pl.CostEstimate(flops=0, bytes_accessed=2**21, transcendentals=0),
        name="query_grad",
    )(term, wide, extra)
    own_rows = lax.all_to_all(rows_out, "head", 0, 0, tiled=True)
    own_rows, _ = lax.optimization_barrier((own_rows, mine))
    steps = bits(n_head)
    for mask in steps[:-1]:
        mine = mine + swap(mine.astype(BF16), "head", n_head, mask).astype(F32)
    last = swap(mine.astype(BF16), "head", n_head, steps[-1])

    all_rows = {0: own_rows}
    for k in range(2, n_seq, 2):
        all_rows[k] = swap(all_rows[0], "seq", n_seq, k)
    for k in range(0, n_seq, 2):
        all_rows[k + 1] = swap(all_rows[k], "seq", n_seq, 1)
    grad_query_index, hw, kl = pl.pallas_call(
        functools.partial(place_kernel, n_seq),
        in_specs=[vmem_spec()] * n_seq,
        out_specs=[pl.BlockSpec(memory_space=pl.ANY)] * 3,
        out_shape=[
            jax.ShapeDtypeStruct((rows, heads * width), BF16),
            jax.ShapeDtypeStruct((heads, rows), BF16),
            jax.ShapeDtypeStruct((rows,), BF16),
        ],
        scratch_shapes=[
            pltpu.VMEM((rows, LANES), F32),
            pltpu.VMEM((heads, rows), BF16),
            pltpu.VMEM((rows,), BF16),
            pltpu.SemaphoreType.DMA((n_seq + 2,)),
        ],
        compiler_params=limit(4),
        cost_estimate=pl.CostEstimate(flops=0, bytes_accessed=8 * rows * wide_cols, transcendentals=0),
        name="place",
    )(*[all_rows[k] for k in range(n_seq)])
    grad_key_index = (mine + last.astype(F32)).astype(BF16)
    return kl, grad_query_index, hw.T, grad_key_index


def plain_local(query_mla, key_mla, lse, query_index, key_index, head_weight, query_pos, key_block):
    row_count = query_mla.shape[0]
    key_count = key_mla.shape[0]
    mla_heads = lse.shape[1]
    head_width = query_mla.shape[1] // mla_heads
    index_heads = head_weight.shape[1]
    index_width = key_index.shape[1]
    queries = query_mla.reshape(row_count, mla_heads, head_width)
    mla_keys = key_mla.reshape(key_count, mla_heads, head_width)
    positions = key_block[0] * key_count + jnp.arange(key_count, dtype=jnp.int32)
    valid = positions[None, :] <= query_pos[:, None]
    score = jnp.einsum(
        "thd,jhd->htj", queries, mla_keys, preferred_element_type=jnp.float32
    ) * head_width ** (-0.5)
    attention_part = jnp.sum(
        jnp.where(valid[None], jnp.exp(score - lse.T[:, :, None]), 0.0), axis=0
    )
    indexer_q = query_index.reshape(row_count, index_heads, index_width)
    dots = jnp.einsum("tid,jd->tij", indexer_q, key_index, preferred_element_type=jnp.float32)
    rectified = jnp.maximum(dots, 0.0)
    logit_part = jnp.sum(head_weight[:, :, None] * rectified, axis=1)
    attention, logit = lax.psum((attention_part, logit_part), "head")
    masked = jnp.where(valid, logit, -1e30)
    local_peak = jnp.max(masked, axis=1)
    peak = lax.pmax(local_peak, "seq")
    shifted = jnp.where(valid, jnp.exp(masked - peak[:, None]), 0.0)
    norm, total = lax.psum((jnp.sum(shifted, axis=1), jnp.sum(attention, axis=1)), "seq")
    target = attention / total[:, None]
    log_prob = masked - peak[:, None] - jnp.log(norm)[:, None]
    prob = jnp.where(valid, jnp.exp(log_prob), 0.0)
    log_target = jnp.log(jnp.where(valid, attention, 1.0)) - jnp.log(total)[:, None]
    kl_part = jnp.sum(jnp.where(valid, target * (log_target - log_prob), 0.0), axis=1)
    dlogit = jnp.where(valid, prob - target, 0.0).astype(jnp.bfloat16)
    grad_rows = dlogit.astype(jnp.float32)
    weight_part = jnp.sum(grad_rows[:, None, :] * rectified, axis=2)
    opened = dots > 0
    gated = jnp.where(opened, dlogit[:, None, :], 0)
    query_part = jnp.einsum(
        "tij,jd->tid", gated, key_index, preferred_element_type=jnp.float32
    ).reshape(row_count, index_heads * index_width)
    coef = jnp.where(opened, grad_rows[:, None, :] * head_weight[:, :, None], 0.0).astype(
        jnp.bfloat16
    )
    key_part = jnp.einsum("tij,tid->jd", coef, indexer_q, preferred_element_type=jnp.float32)
    grad_key_index = lax.psum(key_part, "head").astype(jnp.bfloat16)
    query_sum, weight_sum, kl_sum = lax.psum((query_part, weight_part, kl_part), "seq")
    scaled = query_sum.reshape(row_count, index_heads, index_width) * head_weight[:, :, None]
    grad_query_index = scaled.reshape(row_count, index_heads * index_width).astype(jnp.bfloat16)
    grad_head_weight = weight_sum.astype(jnp.bfloat16)
    kl = kl_sum.astype(jnp.bfloat16)
    return (kl, grad_query_index, grad_head_weight, grad_key_index)


def solution(mesh):
    placed = (
        P(None, "head"),
        P("seq", "head"),
        P(None, "head"),
        P(None, "head"),
        P("seq", None),
        P(None, "head"),
        P(),
        P("seq"),
    )
    n_seq, n_head = mesh.shape["seq"], mesh.shape["head"]

    def local(*args):
        rows, heads = args[0].shape[0], args[5].shape[1]
        paired = all(n & (n - 1) == 0 and n > 1 for n in (n_seq, n_head))
        if paired and rows == 8 * n_seq * n_head and heads % n_seq == 0 and 3 * heads + 3 <= LANES:
            return fast_local(n_seq, n_head, *args)
        return plain_local(*args)

    return jax.shard_map(
        local,
        mesh=mesh,
        in_specs=placed,
        out_specs=(P(), P(None, "head"), P(None, "head"), P("seq", None)),
        check_vma=False,
    )
```
